32 devices in a mesh: blk: 8 (over y, x, core), aux: 4 (over z).
Axes of the slice: x: 2, y: 2, z: 4, core: 2. Of those that a mesh axis runs over, the one named last changes fastest.
Arguments:
- occupied_integrals: float32 [8, 128, 3072], P(None, 'blk', 'aux'), may hold values from -6 to 6
- virtual_coefficients: float32 [128, 384], replicated, may hold values from -0.0625 to 0.0625
- shell_size: int32 [16], replicated, may hold values from 1 to 8, as said below
- shell_owner: int32 [16], replicated, may hold values from 0 to 7, as said below
- occ_owner: int32 [8], replicated, may hold values from 0 to 7, each once
- e_occ: float32 [8], replicated, may hold values from -1.5 to -0.4
- e_virt: float32 [384], replicated, may hold values from 0.3 to 2.5
Outputs:
- density: float32 [8, 384, 3072], P('blk', None, 'aux')
The draws below stay inside these ranges and needn't reach their ends.
Inputs may be any that keep to these rules, and one draw needn't show every extreme that they name: `shell_size`: every shell holds 1 to 8 functions; the shells of one blk index hold at most 16 together, and those of some blk index exactly 16. `shell_owner`: every blk index owns exactly 2 shells. `occ_owner`: each orbital appears once.
All inputs are finite; a program needn't handle non-finite values.
Results may differ from the reference program's by a relative error of at most 0.0003.
Values sent between devices are 32-bit elements; how exact they have to be, the bound alone decides.
No kernel may reach another device: no remote copies, remote signals or barrier semaphores. Data moves between devices by JAX's collectives and lax.ppermute only.
A program may use at most 64 MiB of HBM per device.

```python
import jax
import jax.numpy as jnp
from jax import lax

VIRTUAL_COUNT = 384
AUXILIARY_COUNT = 3072
OCC_DEV = 1
SHELL_MAX = 8
SH_DEV = 2
STOPS = 3
BASIS_SLOT_LIMIT = 16
NSHELL = 16
SLOT_TOTAL = 128
OCCUPIED_COUNT = 8
N_BLK = 8


def shell_tables(key):
    base = jax.random.fold_in(key, 4711)
    key_perm, key_size, key_full = jax.random.split(base, 3)
    owners = NSHELL // SH_DEV
    shuffled = jax.random.permutation(key_perm, jnp.arange(NSHELL, dtype=jnp.int32))
    owner_map = jnp.mod(shuffled, owners).astype(jnp.int32)
    sizes = jax.random.randint(key_size, (NSHELL,), 1, SHELL_MAX + 1).astype(jnp.int32)
    full_owner = jax.random.randint(key_full, (), 0, owners).astype(jnp.int32)
    sizes = jnp.where(owner_map == full_owner, SHELL_MAX, sizes).astype(jnp.int32)
    return (sizes, owner_map)


def draw_shell_size(key, part):
    return shell_tables(key)[0]


def draw_shell_owner(key, part):
    return shell_tables(key)[1]


def block_levels(rng, dims, cuts, smallest, top_value):
    def one(axis_at, blocks):
        heights = jax.random.uniform(jax.random.fold_in(jax.random.fold_in(rng, 6), axis_at), (blocks,), jnp.float32, smallest / len(cuts), top_value / len(cuts))
        return jnp.repeat(jnp.exp(heights), dims[axis_at] // blocks).reshape((-1,) + (1,) * (len(dims) - axis_at - 1))

    level = one(*cuts[0])
    for cut in cuts[1:]:
        level = level * one(*cut)
    return level


def normal_values(key, dims, spread, reach, cuts=(), kind=jnp.bfloat16):
    array = spread * jax.random.normal(key, dims, jnp.float32)
    if cuts:
        array = array * block_levels(key, dims, cuts, -0.22, 0.18)
    return jnp.clip(array, -reach, reach).astype(kind)


def setup_inputs(seed: int = 0) -> dict:
    splits = jax.random.split(jax.random.key(seed), 8)
    return {
        "occupied_integrals": normal_values(splits[0], (OCCUPIED_COUNT, SLOT_TOTAL, AUXILIARY_COUNT), 1.0, 6.0, ((1, 8), (2, 4)), jnp.float32),
        "virtual_coefficients": normal_values(splits[1], (SLOT_TOTAL, VIRTUAL_COUNT), (BASIS_SLOT_LIMIT * N_BLK * AUXILIARY_COUNT // 48) ** -0.5, 0.0625, (), jnp.float32),
        "shell_size": draw_shell_size(jax.random.fold_in(splits[7], 71), 0),
        "shell_owner": draw_shell_owner(jax.random.fold_in(splits[7], 71), 0),
        "occ_owner": jax.random.permutation(splits[4], OCCUPIED_COUNT).astype(jnp.int32),
        "e_occ": jnp.clip(jax.random.uniform(splits[5], (OCCUPIED_COUNT,), jnp.float32, -1.5, -0.4), -1.5, -0.4),
        "e_virt": jnp.clip(jax.random.uniform(splits[6], (VIRTUAL_COUNT,), jnp.float32, 0.3, 2.5), 0.3, 2.5),
    }


def reference(occupied_integrals, virtual_coefficients, shell_size, shell_owner, occ_owner, e_occ, e_virt):
    owner_hits = (shell_owner[:, None] == jnp.arange(N_BLK, dtype=jnp.int32)[None, :]).astype(jnp.int32)
    slot_load = jnp.sum(shell_size[:, None] * owner_hits, axis=0)
    live_mask = (jnp.arange(BASIS_SLOT_LIMIT, dtype=jnp.int32)[None, :] < slot_load[:, None]).astype(jnp.float32)
    masked_coef = virtual_coefficients * live_mask.reshape(-1)[:, None]

    def transform(orbital):
        return jnp.dot(masked_coef.T, occupied_integrals[orbital], precision=lax.Precision.HIGHEST)

    bvec = lax.map(transform, occ_owner)
    blocks = bvec.reshape(N_BLK, OCC_DEV * VIRTUAL_COUNT, AUXILIARY_COUNT)
    block_energy = e_occ[occ_owner].reshape(N_BLK, OCC_DEV)

    def one_block(block_index):
        own_block = lax.dynamic_index_in_dim(blocks, block_index, 0, keepdims=False)
        own_energy = lax.dynamic_index_in_dim(block_energy, block_index, 0, keepdims=False)
        total = jnp.zeros((OCC_DEV * VIRTUAL_COUNT, AUXILIARY_COUNT), jnp.float32)
        for stop in range(STOPS):
            partner_index = jnp.mod(block_index - stop, N_BLK).astype(jnp.int32)
            partner = lax.dynamic_index_in_dim(blocks, partner_index, 0, keepdims=False)
            partner_energy = lax.dynamic_index_in_dim(block_energy, partner_index, 0, keepdims=False)
            pair_ints = jnp.dot(own_block, partner.T, precision=lax.Precision.HIGHEST)
            pair_ints = pair_ints.reshape(OCC_DEV, VIRTUAL_COUNT, OCC_DEV, VIRTUAL_COUNT)
            combined = 2.0 * pair_ints - pair_ints.transpose(0, 3, 2, 1)
            denominator = (own_energy[:, None, None, None] + partner_energy[None, None, :, None]
                           - e_virt[None, :, None, None] - e_virt[None, None, None, :])
            amplitudes = (combined / denominator).reshape(OCC_DEV * VIRTUAL_COUNT, OCC_DEV * VIRTUAL_COUNT)
            total = total + jnp.dot(amplitudes, partner, precision=lax.Precision.HIGHEST)
        return total

    result = lax.map(one_block, jnp.arange(N_BLK, dtype=jnp.int32))
    return result.reshape(OCCUPIED_COUNT, VIRTUAL_COUNT, AUXILIARY_COUNT)
```

```python
import functools

import jax
import jax.numpy as jnp
from jax import lax
from jax.experimental import pallas as pl
from jax.experimental.pallas import tpu as pltpu
from jax.sharding import PartitionSpec as P

STOPS = 3
BF16 = jnp.bfloat16
F32 = jnp.float32


def shifted(value, axis, steps):
    count = lax.axis_size(axis)
    pairs = [(source, (source + steps) % count) for source in range(count)]
    return lax.ppermute(value, axis, pairs)


def live_slots(shell_size, shell_owner, blk_count, slot_cap):
    owner_hits = (shell_owner[:, None] == jnp.arange(blk_count, dtype=jnp.int32)[None, :]).astype(
        jnp.int32
    )
    slot_load = jnp.sum(shell_size[:, None] * owner_hits, axis=0)
    return (jnp.arange(slot_cap, dtype=jnp.int32)[None, :] < slot_load[:, None]).astype(F32)


def transformed_first(
    occupied_integrals, virtual_coefficients, shell_size, shell_owner, occ_owner, e_occ, e_virt
):
    blk_count = lax.axis_size("blk")
    occ_total = occupied_integrals.shape[0]
    slot_cap = occupied_integrals.shape[1]
    aux_width = occupied_integrals.shape[2]
    virt_count = virtual_coefficients.shape[1]
    occ_local = occ_total // blk_count
    pair_rows = occ_local * virt_count
    highest = lax.Precision.HIGHEST
    live_mask = live_slots(shell_size, shell_owner, blk_count, slot_cap)
    masked_coef = (
        virtual_coefficients.reshape(blk_count, slot_cap, virt_count) * live_mask[:, :, None]
    )
    grouped = jnp.take(occupied_integrals, occ_owner, axis=0).reshape(
        blk_count, occ_local, slot_cap, aux_width
    )
    owned = jnp.einsum(
        "dnkq,dkv->nvq",
        lax.all_to_all(grouped, "blk", split_axis=0, concat_axis=0, tiled=True),
        masked_coef,
        precision=highest,
    )
    own_block = owned.reshape(pair_rows, aux_width)
    my_index = lax.axis_index("blk")
    block_energy = jnp.take(e_occ, occ_owner).reshape(blk_count, occ_local)
    own_energy = lax.dynamic_index_in_dim(block_energy, my_index, 0, keepdims=False)
    partners = [own_block]
    partner_energies = [own_energy]
    passing = own_block
    for stop in range(1, STOPS):
        passing = shifted(passing, "blk", 1)
        partners.append(passing)
        partner_index = jnp.mod(my_index - stop, blk_count)
        partner_energies.append(
            lax.dynamic_index_in_dim(block_energy, partner_index, 0, keepdims=False)
        )
    density = jnp.zeros((pair_rows, aux_width), F32)
    for stop in range(STOPS):
        pair_ints = jnp.einsum("rq,cq->rc", own_block, partners[stop], precision=highest)
        pair_ints = pair_ints.reshape(occ_local, virt_count, occ_local, virt_count)
        summed = lax.psum(2.0 * pair_ints - pair_ints.transpose(0, 3, 2, 1), "aux")
        amplitudes = (
            summed
            / (
                own_energy[:, None, None, None]
                + partner_energies[stop][None, None, :, None]
                - e_virt[None, :, None, None]
                - e_virt[None, None, None, :]
            )
        ).reshape(pair_rows, pair_rows)
        density = density + jnp.dot(amplitudes, partners[stop], precision=highest)
    return density.reshape(occ_local, virt_count, aux_width)


def halves(value):
    high = value.astype(BF16)
    return high, (value - high.astype(F32)).astype(BF16)


def matmul(a, b):
    return jnp.dot(a, b, preferred_element_type=F32)


def matmul_nt(a, b):
    return lax.dot_general(a, b, (((1,), (1,)), ((), ())), preferred_element_type=F32)


def coefficient_kernel(coef_ref, left_ref, right_ref, back_ref):
    coef = coef_ref[...]
    high, low = halves(coef)
    right_ref[...] = jnp.concatenate([high, low, high], axis=0)
    turned = coef.T
    high, low = halves(turned)
    left_ref[...] = jnp.concatenate([high, high, low], axis=1)
    back_ref[...] = jnp.concatenate([high, low], axis=1)


def overlap_kernel(parts, slot_cap, place_ref, *refs):
    pieces = refs[: -parts - 3]
    outs = refs[-parts - 3 : -3]
    x_high, x_low, total = refs[-3:]
    first = place_ref[0]
    for stop in range(STOPS):
        for index, piece in enumerate(pieces):
            high, low = halves(piece[first + stop])
            rows = pl.ds((stop * len(pieces) + index) * slot_cap, slot_cap)
            x_high[rows, :] = high
            x_low[rows, :] = low
    slots = slot_cap * len(pieces)
    own_high, own_low = x_high[:slots, :], x_low[:slots, :]
    for stop in range(STOPS):
        rows = pl.ds(stop * slots, slots)
        high = x_high[rows, :]
        gram = (
            matmul_nt(own_high, high)
            + matmul_nt(own_high, x_low[rows, :])
            + matmul_nt(own_low, high)
        )
        if stop > 0:
            gram = 2.0 * gram - gram.T
        total[:, rows] = gram
    share = slots // parts
    for step, out in enumerate(outs):
        row = pl.multiple_of(lax.rem(place_ref[1] + step, parts) * share, share)
        out[...] = total[pl.ds(row, share), :]


def density_kernel(parts, place_ref, energy_ref, *refs):
    shares = refs[:parts]
    e_row, e_col, left, right, back, x_high, x_low, out, total, w_high, w_low = refs[parts:]
    slots = total.shape[0]
    share = slots // parts
    for step, piece in enumerate(shares):
        row = pl.multiple_of(lax.rem(place_ref[1] + parts - step, parts) * share, share)
        total[pl.ds(row, share), :] = piece[...]
    high, low = halves(total[...])
    half_done = matmul(left[...], jnp.concatenate([high, low, high], axis=0))
    for stop in range(STOPS):
        cols = pl.ds(stop * slots, slots)
        high, low = halves(half_done[:, stop * slots : (stop + 1) * slots])
        summed = matmul(jnp.concatenate([high, high, low], axis=1), right[...])
        gap = (energy_ref[0] + energy_ref[stop] - e_col[...]) - e_row[...]
        high, low = halves(summed / gap)
        both = matmul(high, back[...])
        weight = both[:, :slots] + both[:, slots:] + matmul(low, back[:, :slots])
        w_high[:, cols], w_low[:, cols] = halves(weight)
    out[...] = (
        matmul(w_high[...], x_high[...])
        + matmul(w_high[...], x_low[...])
        + matmul(w_low[...], x_high[...])
    )


def slots_first(
    occupied_integrals, virtual_coefficients, shell_size, shell_owner, occ_owner, e_occ, e_virt
):
    blk_count = lax.axis_size("blk")
    parts = lax.axis_size("aux")
    _, slot_cap, aux_width = occupied_integrals.shape
    slots, virt_count = virtual_coefficients.shape
    chips = blk_count // 2
    my_index = lax.axis_index("blk")
    my_chip, my_core = my_index // 2, my_index % 2
    vmem = pl.BlockSpec(memory_space=pltpu.VMEM)
    smem = pl.BlockSpec(memory_space=pltpu.SMEM)

    def other(chip, step):
        return chip ^ step if chips & (chips - 1) == 0 else (chip + step) % chips

    def source(chip, step):
        return chip ^ step if chips & (chips - 1) == 0 else (chip + chips - step) % chips

    window = jnp.arange(STOPS + 1, dtype=jnp.int32)

    def wanted(chip):
        rows = jnp.mod(2 * chip + 1 - window, blk_count)
        return jnp.take(occupied_integrals, jnp.take(occ_owner, rows), axis=0)

    pieces, owners = [], []
    for step in range(chips):
        piece = wanted(other(my_chip, step))
        if step > 0:
            pairs = [
                (2 * chip + core, 2 * other(chip, step) + core)
                for chip in range(chips)
                for core in range(2)
            ]
            piece = lax.ppermute(piece, "blk", pairs)
        swapped = lax.ppermute(piece, "blk", [(i, i ^ 1) for i in range(blk_count)])
        pieces += [piece, swapped]
        owner = 2 * source(my_chip, step)
        owners += [owner + my_core, owner + 1 - my_core]
    owners = jnp.stack(owners)

    live_mask = live_slots(shell_size, shell_owner, blk_count, slot_cap)
    coef = virtual_coefficients.reshape(blk_count, slot_cap, virt_count) * live_mask[:, :, None]
    coef = jnp.take(coef, owners, axis=0).reshape(slots, virt_count)
    left, right, back = pl.pallas_call(
        coefficient_kernel,
        out_shape=[
            jax.ShapeDtypeStruct((virt_count, 3 * slots), BF16),
            jax.ShapeDtypeStruct((3 * slots, virt_count), BF16),
            jax.ShapeDtypeStruct((virt_count, 2 * slots), BF16),
        ],
        in_specs=[vmem],
        out_specs=[vmem] * 3,
    )(coef)

    stops = jnp.arange(STOPS, dtype=jnp.int32)
    energies = jnp.take(e_occ, jnp.take(occ_owner, jnp.mod(my_index - stops, blk_count)))
    place = jnp.stack([1 - my_core, lax.axis_index("aux")]).astype(jnp.int32)

    share = slots // parts
    *shares, x_high, x_low = pl.pallas_call(
        functools.partial(overlap_kernel, parts, slot_cap),
        out_shape=[jax.ShapeDtypeStruct((share, STOPS * slots), F32)] * parts
        + [jax.ShapeDtypeStruct((STOPS * slots, aux_width), BF16)] * 2,
        in_specs=[smem] + [vmem] * len(pieces),
        out_specs=[vmem] * (parts + 2),
        scratch_shapes=[pltpu.VMEM((slots, STOPS * slots), F32)],
    )(place, *pieces)

    mine = shares[0]
    for step in range(1, parts):
        mine = mine + shifted(shares[step], "aux", step)
    gathered = [mine] + [shifted(mine, "aux", step) for step in range(1, parts)]

    density = pl.pallas_call(
        functools.partial(density_kernel, parts),
        out_shape=jax.ShapeDtypeStruct((virt_count, aux_width), F32),
        in_specs=[smem, smem] + [vmem] * (parts + 7),
        out_specs=vmem,
        scratch_shapes=[
            pltpu.VMEM((slots, STOPS * slots), F32),
            pltpu.VMEM((virt_count, STOPS * slots), BF16),
            pltpu.VMEM((virt_count, STOPS * slots), BF16),
        ],
        compiler_params=pltpu.CompilerParams(vmem_limit_bytes=32 * 1024 * 1024),
    )(
        place,
        energies,
        *gathered,
        e_virt.reshape(1, virt_count),
        e_virt.reshape(virt_count, 1),
        left,
        right,
        back,
        x_high,
        x_low,
    )
    return density.reshape(1, virt_count, aux_width)


def per_device(occupied_integrals, virtual_coefficients, *rest):
    blk_count = lax.axis_size("blk")
    slots, virt_count = virtual_coefficients.shape
    paired = blk_count % 2 == 0 and blk_count == occupied_integrals.shape[0]
    shared = slots % (lax.axis_size("aux") * 16) == 0 and slots <= virt_count
    run = slots_first if paired and shared else transformed_first
    return run(occupied_integrals, virtual_coefficients, *rest)


def solution(mesh):
    in_specs = (P(None, "blk", "aux"), P(), P(), P(), P(), P(), P())
    out_specs = P("blk", None, "aux")
    return jax.shard_map(
        per_device, mesh=mesh, in_specs=in_specs, out_specs=out_specs, check_vma=False
    )
```

```python
import functools

import jax
import jax.numpy as jnp
from jax import lax
from jax.experimental import pallas as pl
from jax.experimental.pallas import tpu as pltpu
from jax.sharding import PartitionSpec as P

STOPS = 3
BF16 = jnp.bfloat16
F32 = jnp.float32
SELECT_VMEM = 24 * 1024 * 1024


def shifted(value, axis, steps):
    count = lax.axis_size(axis)
    pairs = [(source, (source + steps) % count) for source in range(count)]
    return lax.ppermute(value, axis, pairs)


def live_slots(shell_size, shell_owner, blk_count, slot_cap):
    owner_hits = (shell_owner[:, None] == jnp.arange(blk_count, dtype=jnp.int32)[None, :]).astype(
        jnp.int32
    )
    slot_load = jnp.sum(shell_size[:, None] * owner_hits, axis=0)
    return (jnp.arange(slot_cap, dtype=jnp.int32)[None, :] < slot_load[:, None]).astype(F32)


def transformed_first(
    occupied_integrals, virtual_coefficients, shell_size, shell_owner, occ_owner, e_occ, e_virt
):
    blk_count = lax.axis_size("blk")
    occ_total = occupied_integrals.shape[0]
    slot_cap = occupied_integrals.shape[1]
    aux_width = occupied_integrals.shape[2]
    virt_count = virtual_coefficients.shape[1]
    occ_local = occ_total // blk_count
    pair_rows = occ_local * virt_count
    highest = lax.Precision.HIGHEST
    live_mask = live_slots(shell_size, shell_owner, blk_count, slot_cap)
    masked_coef = (
        virtual_coefficients.reshape(blk_count, slot_cap, virt_count) * live_mask[:, :, None]
    )
    grouped = jnp.take(occupied_integrals, occ_owner, axis=0).reshape(
        blk_count, occ_local, slot_cap, aux_width
    )
    owned = jnp.einsum(
        "dnkq,dkv->nvq",
        lax.all_to_all(grouped, "blk", split_axis=0, concat_axis=0, tiled=True),
        masked_coef,
        precision=highest,
    )
    own_block = owned.reshape(pair_rows, aux_width)
    my_index = lax.axis_index("blk")
    block_energy = jnp.take(e_occ, occ_owner).reshape(blk_count, occ_local)
    own_energy = lax.dynamic_index_in_dim(block_energy, my_index, 0, keepdims=False)
    partners = [own_block]
    partner_energies = [own_energy]
    passing = own_block
    for stop in range(1, STOPS):
        passing = shifted(passing, "blk", 1)
        partners.append(passing)
        partner_index = jnp.mod(my_index - stop, blk_count)
        partner_energies.append(
            lax.dynamic_index_in_dim(block_energy, partner_index, 0, keepdims=False)
        )
    density = jnp.zeros((pair_rows, aux_width), F32)
    for stop in range(STOPS):
        pair_ints = jnp.einsum("rq,cq->rc", own_block, partners[stop], precision=highest)
        pair_ints = pair_ints.reshape(occ_local, virt_count, occ_local, virt_count)
        summed = lax.psum(2.0 * pair_ints - pair_ints.transpose(0, 3, 2, 1), "aux")
        amplitudes = (
            summed
            / (
                own_energy[:, None, None, None]
                + partner_energies[stop][None, None, :, None]
                - e_virt[None, :, None, None]
                - e_virt[None, None, None, :]
            )
        ).reshape(pair_rows, pair_rows)
        density = density + jnp.dot(amplitudes, partners[stop], precision=highest)
    return density.reshape(occ_local, virt_count, aux_width)


def halves(value):
    high = value.astype(BF16)
    return high, (value - high.astype(F32)).astype(BF16)


def matmul(a, b):
    return jnp.dot(a, b, preferred_element_type=F32)


def matmul_nt(a, b):
    return lax.dot_general(a, b, (((1,), (1,)), ((), ())), preferred_element_type=F32)


def partner_chip(chip, step, chips):
    return chip ^ step if chips & (chips - 1) == 0 else lax.rem(chip + step, chips)


def source_chip(chip, step, chips):
    return chip ^ step if chips & (chips - 1) == 0 else lax.rem(chip + chips - step, chips)


def select_kernel(blk_count, owner_hbm, x_hbm, *refs):
    *outs, owner_ref, x_ref, owner_sem, x_sem = refs
    chips = blk_count // 2
    my_chip = lax.axis_index("blk") >> 1
    reads = [
        pltpu.make_async_copy(owner_hbm, owner_ref, owner_sem),
        pltpu.make_async_copy(x_hbm, x_ref, x_sem),
    ]
    for read in reads:
        read.start()
    for read in reads:
        read.wait()
    for step, out in enumerate(outs):
        last = 2 * partner_chip(my_chip, step, chips) + 1
        for stop in range(STOPS + 1):
            out[stop] = x_ref[owner_ref[lax.rem(last + blk_count - stop, blk_count)]]


def coefficient_kernel(
    blk_count,
    size_ref,
    shell_ref,
    owner_ref,
    energy_ref,
    coef_ref,
    virt_ref,
    left_ref,
    right_ref,
    back_ref,
    gap_ref,
    ordered,
):
    slots = coef_ref.shape[0]
    slot_cap = slots // blk_count
    me = lax.axis_index("blk")
    shells = [(size_ref[s], shell_ref[s]) for s in range(size_ref.shape[0])]
    count = lax.broadcasted_iota(jnp.int32, (slot_cap, coef_ref.shape[1]), 0)
    for index in range(blk_count):
        chip = source_chip(me >> 1, index // 2, blk_count // 2)
        blk = 2 * chip + ((me & 1) ^ (index % 2))
        load = jnp.int32(0)
        for size, shell in shells:
            load = load + jnp.where(shell == blk, size, 0)
        rows = coef_ref[pl.ds(pl.multiple_of(blk * slot_cap, slot_cap), slot_cap), :]
        ordered[pl.ds(index * slot_cap, slot_cap), :] = jnp.where(count < load, rows, 0.0)
    coef = ordered[...]
    high, low = halves(coef)
    right_ref[...] = jnp.concatenate([high, low, high], axis=0)
    turned = coef.T
    high, low = halves(turned)
    left_ref[...] = jnp.concatenate([high, high, low], axis=1)
    back_ref[...] = jnp.concatenate([high, low], axis=1)
    row = virt_ref[...]
    virt_count = row.shape[1]
    column = jnp.broadcast_to(row, (8, virt_count)).T[:, :1]
    own = energy_ref[owner_ref[me]]
    for stop in range(STOPS):
        both = own + energy_ref[owner_ref[lax.rem(me + blk_count - stop, blk_count)]]
        gap_ref[pl.ds(stop * virt_count, virt_count), :] = 1.0 / ((both - column) - row)


def overlap_kernel(parts, slot_cap, *refs):
    pieces = refs[: -parts - 3]
    outs = refs[-parts - 3 : -3]
    x_high, x_low, total = refs[-3:]
    first = 1 - (lax.axis_index("blk") & 1)
    here = lax.axis_index("aux")
    for stop in range(STOPS):
        for index, piece in enumerate(pieces):
            high, low = halves(piece[first + stop])
            rows = pl.ds((stop * len(pieces) + index) * slot_cap, slot_cap)
            x_high[rows, :] = high
            x_low[rows, :] = low
    slots = slot_cap * len(pieces)
    own_high, own_low = x_high[:slots, :], x_low[:slots, :]
    for stop in range(STOPS):
        rows = pl.ds(stop * slots, slots)
        high = x_high[rows, :]
        gram = (
            matmul_nt(own_high, high)
            + matmul_nt(own_high, x_low[rows, :])
            + matmul_nt(own_low, high)
        )
        if stop > 0:
            gram = 2.0 * gram - gram.T
        total[:, rows] = gram
    share = slots // parts
    for step, out in enumerate(outs):
        row = pl.multiple_of(lax.rem(here + step, parts) * share, share)
        out[...] = total[pl.ds(row, share), :]


def density_kernel(parts, *refs):
    shares = refs[:parts]
    left, right, back, gap, x_high, x_low, out, total, w_high, w_low, density, sems = refs[parts:]
    here = lax.axis_index("aux")
    slots = total.shape[0]
    share = slots // parts
    virt_count = out.shape[0]
    for step, piece in enumerate(shares):
        row = pl.multiple_of(lax.rem(here + parts - step, parts) * share, share)
        total[pl.ds(row, share), :] = piece[...]
    high, low = halves(total[...])
    half_done = matmul(left[...], jnp.concatenate([high, low, high], axis=0))
    half_done = jnp.concatenate(
        [half_done[:, stop * slots : (stop + 1) * slots] for stop in range(STOPS)], axis=0
    )
    high, low = halves(half_done)
    summed = matmul(jnp.concatenate([high, high, low], axis=1), right[...])
    high, low = halves(summed * gap[...])
    both = matmul(high, back[...])
    weight = both[:, :slots] + both[:, slots:] + matmul(low, back[:, :slots])
    for stop in range(STOPS):
        rows = slice(stop * virt_count, (stop + 1) * virt_count)
        cols = slice(stop * slots, (stop + 1) * slots)
        w_high[:, cols], w_low[:, cols] = halves(weight[rows])
    copies = []
    for index in range(sems.shape[0]):
        band = virt_count // sems.shape[0]
        rows = pl.ds(index * band, band)
        high, low = w_high[rows, :], w_low[rows, :]
        x_all = jnp.concatenate([x_high[...], x_high[...], x_low[...]], axis=0)
        density[rows, :] = matmul(jnp.concatenate([high, low, high], axis=1), x_all)
        copies.append(pltpu.make_async_copy(density.at[rows], out.at[rows], sems.at[index]))
        copies[-1].start()
    for copy in copies:
        copy.wait()


def slots_first(
    occupied_integrals, virtual_coefficients, shell_size, shell_owner, occ_owner, e_occ, e_virt
):
    blk_count = lax.axis_size("blk")
    parts = lax.axis_size("aux")
    _, slot_cap, aux_width = occupied_integrals.shape
    slots, virt_count = virtual_coefficients.shape
    chips = blk_count // 2
    vmem = pl.BlockSpec(memory_space=pltpu.VMEM)
    smem = pl.BlockSpec(memory_space=pltpu.SMEM)
    params = pltpu.CompilerParams(vmem_limit_bytes=24 * 1024 * 1024)

    sent = pl.pallas_call(
        functools.partial(select_kernel, blk_count),
        out_shape=[jax.ShapeDtypeStruct((STOPS + 1, slot_cap, aux_width), F32)] * chips,
        in_specs=[pl.BlockSpec(memory_space=pltpu.HBM)] * 2,
        out_specs=[vmem] * chips,
        scratch_shapes=[
            pltpu.SMEM(occ_owner.shape, jnp.int32),
            pltpu.VMEM(occupied_integrals.shape, F32),
            pltpu.SemaphoreType.DMA,
            pltpu.SemaphoreType.DMA,
        ],
        compiler_params=pltpu.CompilerParams(vmem_limit_bytes=SELECT_VMEM),
    )(occ_owner, occupied_integrals)

    pieces = []
    for step, piece in enumerate(sent):
        if step > 0:
            pairs = [
                (2 * chip + core, 2 * int(partner_chip(chip, step, chips)) + core)
                for chip in range(chips)
                for core in range(2)
            ]
            piece = lax.ppermute(piece, "blk", pairs)
        pieces += [piece, lax.ppermute(piece, "blk", [(i, i ^ 1) for i in range(blk_count)])]

    left, right, back, gap = pl.pallas_call(
        functools.partial(coefficient_kernel, blk_count),
        out_shape=[
            jax.ShapeDtypeStruct((virt_count, 3 * slots), BF16),
            jax.ShapeDtypeStruct((3 * slots, virt_count), BF16),
            jax.ShapeDtypeStruct((virt_count, 2 * slots), BF16),
            jax.ShapeDtypeStruct((STOPS * virt_count, virt_count), F32),
        ],
        in_specs=[smem] * 4 + [vmem] * 2,
        out_specs=[vmem] * 4,
        scratch_shapes=[pltpu.VMEM((slots, virt_count), F32)],
        compiler_params=params,
    )(
        shell_size,
        shell_owner,
        occ_owner,
        e_occ,
        virtual_coefficients,
        e_virt.reshape(1, virt_count),
    )

    share = slots // parts
    *shares, x_high, x_low = pl.pallas_call(
        functools.partial(overlap_kernel, parts, slot_cap),
        out_shape=[jax.ShapeDtypeStruct((share, STOPS * slots), F32)] * parts
        + [jax.ShapeDtypeStruct((STOPS * slots, aux_width), BF16)] * 2,
        in_specs=[vmem] * len(pieces),
        out_specs=[vmem] * (parts + 2),
        scratch_shapes=[pltpu.VMEM((slots, STOPS * slots), F32)],
        compiler_params=params,
    )(*pieces)

    mine = shares[0]
    for step in range(1, parts):
        mine = mine + shifted(shares[step], "aux", step)
    gathered = [mine] + [shifted(mine, "aux", step) for step in range(1, parts)]

    bands = 3 if virt_count % 48 == 0 else 1
    density = pl.pallas_call(
        functools.partial(density_kernel, parts),
        out_shape=jax.ShapeDtypeStruct((virt_count, aux_width), F32),
        in_specs=[vmem] * (parts + 6),
        out_specs=pl.BlockSpec(memory_space=pl.ANY),
        scratch_shapes=[
            pltpu.VMEM((slots, STOPS * slots), F32),
            pltpu.VMEM((virt_count, STOPS * slots), BF16),
            pltpu.VMEM((virt_count, STOPS * slots), BF16),
            pltpu.VMEM((virt_count, aux_width), F32),
            pltpu.SemaphoreType.DMA((bands,)),
        ],
        compiler_params=params,
    )(*gathered, left, right, back, gap, x_high, x_low)
    return density.reshape(1, virt_count, aux_width)


def per_device(occupied_integrals, virtual_coefficients, *rest):
    blk_count = lax.axis_size("blk")
    slots, virt_count = virtual_coefficients.shape
    paired = blk_count % 2 == 0 and blk_count == occupied_integrals.shape[0]
    shared = slots % (lax.axis_size("aux") * 16) == 0 and slots <= virt_count
    run = slots_first if paired and shared else transformed_first
    return run(occupied_integrals, virtual_coefficients, *rest)


def solution(mesh):
    in_specs = (P(None, "blk", "aux"), P(), P(), P(), P(), P(), P())
    out_specs = P("blk", None, "aux")
    return jax.shard_map(
        per_device, mesh=mesh, in_specs=in_specs, out_specs=out_specs, check_vma=False
    )
```

```python
import functools

import jax
import jax.numpy as jnp
from jax import lax
from jax.experimental import pallas as pl
from jax.experimental.pallas import tpu as pltpu
from jax.sharding import PartitionSpec as P

STOPS = 3
BF16 = jnp.bfloat16
F32 = jnp.float32


def shifted(value, axis, steps):
    count = lax.axis_size(axis)
    pairs = [(source, (source + steps) % count) for source in range(count)]
    return lax.ppermute(value, axis, pairs)


def swapped(value, axis, step):
    return lax.ppermute(value, axis, [(i, i ^ step) for i in range(lax.axis_size(axis))])


def live_slots(shell_size, shell_owner, blk_count, slot_cap):
    owner_hits = (shell_owner[:, None] == jnp.arange(blk_count, dtype=jnp.int32)[None, :]).astype(
        jnp.int32
    )
    slot_load = jnp.sum(shell_size[:, None] * owner_hits, axis=0)
    return (jnp.arange(slot_cap, dtype=jnp.int32)[None, :] < slot_load[:, None]).astype(F32)


def transformed_first(
    occupied_integrals, virtual_coefficients, shell_size, shell_owner, occ_owner, e_occ, e_virt
):
    blk_count = lax.axis_size("blk")
    occ_total = occupied_integrals.shape[0]
    slot_cap = occupied_integrals.shape[1]
    aux_width = occupied_integrals.shape[2]
    virt_count = virtual_coefficients.shape[1]
    occ_local = occ_total // blk_count
    pair_rows = occ_local * virt_count
    highest = lax.Precision.HIGHEST
    live_mask = live_slots(shell_size, shell_owner, blk_count, slot_cap)
    masked_coef = (
        virtual_coefficients.reshape(blk_count, slot_cap, virt_count) * live_mask[:, :, None]
    )
    grouped = jnp.take(occupied_integrals, occ_owner, axis=0).reshape(
        blk_count, occ_local, slot_cap, aux_width
    )
    owned = jnp.einsum(
        "dnkq,dkv->nvq",
        lax.all_to_all(grouped, "blk", split_axis=0, concat_axis=0, tiled=True),
        masked_coef,
        precision=highest,
    )
    own_block = owned.reshape(pair_rows, aux_width)
    my_index = lax.axis_index("blk")
    block_energy = jnp.take(e_occ, occ_owner).reshape(blk_count, occ_local)
    own_energy = lax.dynamic_index_in_dim(block_energy, my_index, 0, keepdims=False)
    partners = [own_block]
    partner_energies = [own_energy]
    passing = own_block
    for stop in range(1, STOPS):
        passing = shifted(passing, "blk", 1)
        partners.append(passing)
        partner_index = jnp.mod(my_index - stop, blk_count)
        partner_energies.append(
            lax.dynamic_index_in_dim(block_energy, partner_index, 0, keepdims=False)
        )
    density = jnp.zeros((pair_rows, aux_width), F32)
    for stop in range(STOPS):
        pair_ints = jnp.einsum("rq,cq->rc", own_block, partners[stop], precision=highest)
        pair_ints = pair_ints.reshape(occ_local, virt_count, occ_local, virt_count)
        summed = lax.psum(2.0 * pair_ints - pair_ints.transpose(0, 3, 2, 1), "aux")
        amplitudes = (
            summed
            / (
                own_energy[:, None, None, None]
                + partner_energies[stop][None, None, :, None]
                - e_virt[None, :, None, None]
                - e_virt[None, None, None, :]
            )
        ).reshape(pair_rows, pair_rows)
        density = density + jnp.dot(amplitudes, partners[stop], precision=highest)
    return density.reshape(occ_local, virt_count, aux_width)


def halves(value):
    high = value.astype(BF16)
    return high, (value - high.astype(F32)).astype(BF16)


def matmul(a, b):
    return jnp.dot(a, b, preferred_element_type=F32)


def matmul_nt(a, b):
    return lax.dot_general(a, b, (((1,), (1,)), ((), ())), preferred_element_type=F32)


def partner_chip(chip, step, chips):
    return chip ^ step if chips & (chips - 1) == 0 else lax.rem(chip + step, chips)


def source_chip(chip, step, chips):
    return chip ^ step if chips & (chips - 1) == 0 else lax.rem(chip + chips - step, chips)


def select_kernel(blk_count, owner_hbm, x_hbm, *refs):
    *outs, owner_ref, x_ref, owner_sem, x_sem = refs
    chips = blk_count // 2
    my_chip = lax.axis_index("blk") >> 1
    reads = [
        pltpu.make_async_copy(owner_hbm, owner_ref, owner_sem),
        pltpu.make_async_copy(x_hbm, x_ref, x_sem),
    ]
    for read in reads:
        read.start()
    for read in reads:
        read.wait()
    for step, out in enumerate(outs):
        last = 2 * partner_chip(my_chip, step, chips) + 1
        for stop in range(STOPS + 1):
            out[stop] = x_ref[owner_ref[lax.rem(last + blk_count - stop, blk_count)]]


def coefficient_kernel(
    blk_count,
    size_ref,
    shell_ref,
    owner_ref,
    energy_ref,
    coef_ref,
    virt_ref,
    left_ref,
    right_ref,
    back_ref,
    gap_ref,
    ordered,
):
    slots = coef_ref.shape[0]
    slot_cap = slots // blk_count
    me = lax.axis_index("blk")
    shells = [(size_ref[s], shell_ref[s]) for s in range(size_ref.shape[0])]
    count = lax.broadcasted_iota(jnp.int32, (slot_cap, coef_ref.shape[1]), 0)
    for index in range(blk_count):
        chip = source_chip(me >> 1, index // 2, blk_count // 2)
        blk = 2 * chip + ((me & 1) ^ (index % 2))
        load = jnp.int32(0)
        for size, shell in shells:
            load = load + jnp.where(shell == blk, size, 0)
        rows = coef_ref[pl.ds(pl.multiple_of(blk * slot_cap, slot_cap), slot_cap), :]
        ordered[pl.ds(index * slot_cap, slot_cap), :] = jnp.where(count < load, rows, 0.0)
    coef = ordered[...]
    high, low = halves(coef)
    right_ref[...] = jnp.concatenate([high, low, high], axis=0)
    turned = coef.T
    high, low = halves(turned)
    left_ref[...] = jnp.concatenate([high, high, low], axis=1)
    back_ref[...] = jnp.concatenate([high, low], axis=1)
    row = virt_ref[...]
    virt_count = row.shape[1]
    column = jnp.broadcast_to(row, (8, virt_count)).T[:, :1]
    own = energy_ref[owner_ref[me]]
    for stop in range(STOPS):
        both = own + energy_ref[owner_ref[lax.rem(me + blk_count - stop, blk_count)]]
        gap_ref[pl.ds(stop * virt_count, virt_count), :] = 1.0 / ((both - column) - row)


def overlap_kernel(slot_cap, places, *refs):
    *pieces, keep, give, x_high, x_low, total = refs
    first = 1 - (lax.axis_index("blk") & 1)
    here = lax.axis_index("aux")
    for stop in range(STOPS):
        for index, piece in zip(places, pieces):
            high, low = halves(piece[first + stop])
            rows = pl.ds((stop * len(pieces) + index) * slot_cap, slot_cap)
            x_high[rows, :] = high
            x_low[rows, :] = low
    slots = slot_cap * len(pieces)
    own_high, own_low = x_high[:slots, :], x_low[:slots, :]
    for stop in range(STOPS):
        rows = pl.ds(stop * slots, slots)
        high = x_high[rows, :]
        gram = (
            matmul_nt(own_high, high)
            + matmul_nt(own_high, x_low[rows, :])
            + matmul_nt(own_low, high)
        )
        if stop > 0:
            gram = 2.0 * gram - gram.T
        total[:, rows] = gram
    half = slots // 2
    mine = here & 1
    keep[...] = total[pl.ds(pl.multiple_of(mine * half, half), half), :]
    give[...] = total[pl.ds(pl.multiple_of((1 - mine) * half, half), half), :]


def density_kernel(steps, *refs):
    parts = len(steps)
    shares = refs[:parts]
    left, right, back, gap, x_high, x_low, out, total, w_high, w_low, density, sems = refs[parts:]
    here = lax.axis_index("aux")
    slots = total.shape[0]
    half = slots // 2
    virt_count = out.shape[0]
    for other in range(2):
        row = pl.multiple_of((here & 1 ^ other) * half, half)
        total[pl.ds(row, half), :] = sum(
            piece[...] for step, piece in zip(steps, shares) if step & 1 == other
        )
    high, low = halves(total[...])
    half_done = matmul(left[...], jnp.concatenate([high, low, high], axis=0))
    half_done = jnp.concatenate(
        [half_done[:, stop * slots : (stop + 1) * slots] for stop in range(STOPS)], axis=0
    )
    high, low = halves(half_done)
    summed = matmul(jnp.concatenate([high, high, low], axis=1), right[...])
    high, low = halves(summed * gap[...])
    both = matmul(high, back[...])
    weight = both[:, :slots] + both[:, slots:] + matmul(low, back[:, :slots])
    for stop in range(STOPS):
        rows = slice(stop * virt_count, (stop + 1) * virt_count)
        cols = slice(stop * slots, (stop + 1) * slots)
        w_high[:, cols], w_low[:, cols] = halves(weight[rows])
    copies = []
    for index in range(sems.shape[0]):
        band = virt_count // sems.shape[0]
        rows = pl.ds(index * band, band)
        high, low = w_high[rows, :], w_low[rows, :]
        x_all = jnp.concatenate([x_high[...], x_high[...], x_low[...]], axis=0)
        density[rows, :] = matmul(jnp.concatenate([high, low, high], axis=1), x_all)
        copies.append(pltpu.make_async_copy(density.at[rows], out.at[rows], sems.at[index]))
        copies[-1].start()
    for copy in copies:
        copy.wait()


def slots_first(
    occupied_integrals, virtual_coefficients, shell_size, shell_owner, occ_owner, e_occ, e_virt
):
    blk_count = lax.axis_size("blk")
    parts = lax.axis_size("aux")
    _, slot_cap, aux_width = occupied_integrals.shape
    slots, virt_count = virtual_coefficients.shape
    chips = blk_count // 2
    vmem = pl.BlockSpec(memory_space=pltpu.VMEM)
    smem = pl.BlockSpec(memory_space=pltpu.SMEM)
    params = pltpu.CompilerParams(vmem_limit_bytes=24 * 1024 * 1024)

    sent = pl.pallas_call(
        functools.partial(select_kernel, blk_count),
        out_shape=[jax.ShapeDtypeStruct((STOPS + 1, slot_cap, aux_width), F32)] * chips,
        in_specs=[pl.BlockSpec(memory_space=pltpu.HBM)] * 2,
        out_specs=[vmem] * chips,
        scratch_shapes=[
            pltpu.SMEM(occ_owner.shape, jnp.int32),
            pltpu.VMEM(occupied_integrals.shape, F32),
            pltpu.SemaphoreType.DMA,
            pltpu.SemaphoreType.DMA,
        ],
        compiler_params=params,
    )(*[pltpu.with_memory_space_constraint(a, pltpu.HBM) for a in (occ_owner, occupied_integrals)])

    pieces = []
    for step, piece in enumerate(sent):
        if step > 0:
            pairs = [
                (2 * chip + core, 2 * int(partner_chip(chip, step, chips)) + core)
                for chip in range(chips)
                for core in range(2)
            ]
            piece = lax.ppermute(piece, "blk", pairs)
        pieces += [piece, swapped(piece, "blk", 1)]

    left, right, back, gap = pl.pallas_call(
        functools.partial(coefficient_kernel, blk_count),
        out_shape=[
            jax.ShapeDtypeStruct((virt_count, 3 * slots), BF16),
            jax.ShapeDtypeStruct((3 * slots, virt_count), BF16),
            jax.ShapeDtypeStruct((virt_count, 2 * slots), BF16),
            jax.ShapeDtypeStruct((STOPS * virt_count, virt_count), F32),
        ],
        in_specs=[smem] * 4 + [vmem] * 2,
        out_specs=[vmem] * 4,
        scratch_shapes=[pltpu.VMEM((slots, virt_count), F32)],
        compiler_params=params,
    )(
        shell_size,
        shell_owner,
        occ_owner,
        e_occ,
        virtual_coefficients,
        e_virt.reshape(1, virt_count),
    )

    places = [2 * step + core for step in reversed(range(chips)) for core in range(2)]
    keep, give, x_high, x_low = pl.pallas_call(
        functools.partial(overlap_kernel, slot_cap, places),
        out_shape=[jax.ShapeDtypeStruct((slots // 2, STOPS * slots), F32)] * 2
        + [jax.ShapeDtypeStruct((STOPS * slots, aux_width), BF16)] * 2,
        in_specs=[vmem] * len(pieces),
        out_specs=[vmem] * 4,
        scratch_shapes=[pltpu.VMEM((slots, STOPS * slots), F32)],
        compiler_params=params,
    )(*[pieces[place] for place in places])

    mine = keep + swapped(give, "aux", 1)
    steps = [0, *range(1, parts, 2), *range(2, parts, 2)]
    gathered = [swapped(mine, "aux", step) if step else mine for step in steps]

    bands = 3 if virt_count % 48 == 0 else 1
    density = pl.pallas_call(
        functools.partial(density_kernel, steps),
        out_shape=jax.ShapeDtypeStruct((virt_count, aux_width), F32),
        in_specs=[vmem] * (parts + 6),
        out_specs=pl.BlockSpec(memory_space=pl.ANY),
        scratch_shapes=[
            pltpu.VMEM((slots, STOPS * slots), F32),
            pltpu.VMEM((virt_count, STOPS * slots), BF16),
            pltpu.VMEM((virt_count, STOPS * slots), BF16),
            pltpu.VMEM((virt_count, aux_width), F32),
            pltpu.SemaphoreType.DMA((bands,)),
        ],
        compiler_params=params,
    )(*gathered, left, right, back, gap, x_high, x_low)
    return density.reshape(1, virt_count, aux_width)


def per_device(occupied_integrals, virtual_coefficients, *rest):
    blk_count = lax.axis_size("blk")
    slots, virt_count = virtual_coefficients.shape
    paired = blk_count % 2 == 0 and blk_count == occupied_integrals.shape[0]
    parts = lax.axis_size("aux")
    shared = parts > 1 and parts & (parts - 1) == 0 and slots % 32 == 0 and slots <= virt_count
    run = slots_first if paired and shared else transformed_first
    return run(occupied_integrals, virtual_coefficients, *rest)


def solution(mesh):
    in_specs = (P(None, "blk", "aux"), P(), P(), P(), P(), P(), P())
    out_specs = P("blk", None, "aux")
    return jax.shard_map(
        per_device, mesh=mesh, in_specs=in_specs, out_specs=out_specs, check_vma=False
    )
```

```python
import functools

import jax
import jax.numpy as jnp
from jax import lax
from jax.experimental import pallas as pl
from jax.experimental.pallas import tpu as pltpu
from jax.sharding import PartitionSpec as P

STOPS = 3
BF16 = jnp.bfloat16
F32 = jnp.float32


def shifted(value, axis, steps):
    count = lax.axis_size(axis)
    pairs = [(source, (source + steps) % count) for source in range(count)]
    return lax.ppermute(value, axis, pairs)


def swapped(value, axis, step):
    return lax.ppermute(value, axis, [(i, i ^ step) for i in range(lax.axis_size(axis))])


def live_slots(shell_size, shell_owner, blk_count, slot_cap):
    owner_hits = (shell_owner[:, None] == jnp.arange(blk_count, dtype=jnp.int32)[None, :]).astype(
        jnp.int32
    )
    slot_load = jnp.sum(shell_size[:, None] * owner_hits, axis=0)
    return (jnp.arange(slot_cap, dtype=jnp.int32)[None, :] < slot_load[:, None]).astype(F32)


def transformed_first(
    occupied_integrals, virtual_coefficients, shell_size, shell_owner, occ_owner, e_occ, e_virt
):
    blk_count = lax.axis_size("blk")
    occ_total = occupied_integrals.shape[0]
    slot_cap = occupied_integrals.shape[1]
    aux_width = occupied_integrals.shape[2]
    virt_count = virtual_coefficients.shape[1]
    occ_local = occ_total // blk_count
    pair_rows = occ_local * virt_count
    highest = lax.Precision.HIGHEST
    live_mask = live_slots(shell_size, shell_owner, blk_count, slot_cap)
    masked_coef = (
        virtual_coefficients.reshape(blk_count, slot_cap, virt_count) * live_mask[:, :, None]
    )
    grouped = jnp.take(occupied_integrals, occ_owner, axis=0).reshape(
        blk_count, occ_local, slot_cap, aux_width
    )
    owned = jnp.einsum(
        "dnkq,dkv->nvq",
        lax.all_to_all(grouped, "blk", split_axis=0, concat_axis=0, tiled=True),
        masked_coef,
        precision=highest,
    )
    own_block = owned.reshape(pair_rows, aux_width)
    my_index = lax.axis_index("blk")
    block_energy = jnp.take(e_occ, occ_owner).reshape(blk_count, occ_local)
    own_energy = lax.dynamic_index_in_dim(block_energy, my_index, 0, keepdims=False)
    partners = [own_block]
    partner_energies = [own_energy]
    passing = own_block
    for stop in range(1, STOPS):
        passing = shifted(passing, "blk", 1)
        partners.append(passing)
        partner_index = jnp.mod(my_index - stop, blk_count)
        partner_energies.append(
            lax.dynamic_index_in_dim(block_energy, partner_index, 0, keepdims=False)
        )
    density = jnp.zeros((pair_rows, aux_width), F32)
    for stop in range(STOPS):
        pair_ints = jnp.einsum("rq,cq->rc", own_block, partners[stop], precision=highest)
        pair_ints = pair_ints.reshape(occ_local, virt_count, occ_local, virt_count)
        summed = lax.psum(2.0 * pair_ints - pair_ints.transpose(0, 3, 2, 1), "aux")
        amplitudes = (
            summed
            / (
                own_energy[:, None, None, None]
                + partner_energies[stop][None, None, :, None]
                - e_virt[None, :, None, None]
                - e_virt[None, None, None, :]
            )
        ).reshape(pair_rows, pair_rows)
        density = density + jnp.dot(amplitudes, partners[stop], precision=highest)
    return density.reshape(occ_local, virt_count, aux_width)


def halves(value):
    high = value.astype(BF16)
    return high, (value - high.astype(F32)).astype(BF16)


def matmul(a, b):
    return jnp.dot(a, b, preferred_element_type=F32)


def matmul_nt(a, b):
    return lax.dot_general(a, b, (((1,), (1,)), ((), ())), preferred_element_type=F32)


def partner_chip(chip, step, chips):
    return chip ^ step if chips & (chips - 1) == 0 else lax.rem(chip + step, chips)


def source_chip(chip, step, chips):
    return chip ^ step if chips & (chips - 1) == 0 else lax.rem(chip + chips - step, chips)


def select_kernel(blk_count, owner_hbm, x_hbm, *refs):
    *outs, owner_ref, x_ref, owner_sem, x_sem = refs
    chips = blk_count // 2
    my_chip = lax.axis_index("blk") >> 1
    reads = [
        pltpu.make_async_copy(owner_hbm, owner_ref, owner_sem),
        pltpu.make_async_copy(x_hbm, x_ref, x_sem),
    ]
    for read in reads:
        read.start()
    for read in reads:
        read.wait()
    for step, out in enumerate(outs):
        last = 2 * partner_chip(my_chip, step, chips) + 1
        for stop in range(STOPS + 1):
            out[stop] = x_ref[owner_ref[lax.rem(last + blk_count - stop, blk_count)]]


def coefficient_kernel(
    blk_count,
    size_ref,
    shell_ref,
    owner_ref,
    energy_ref,
    coef_ref,
    virt_ref,
    left_ref,
    right_ref,
    back_ref,
    gap_ref,
    ordered,
):
    slots = coef_ref.shape[0]
    slot_cap = slots // blk_count
    me = lax.axis_index("blk")
    shells = [(size_ref[s], shell_ref[s]) for s in range(size_ref.shape[0])]
    count = lax.broadcasted_iota(jnp.int32, (slot_cap, coef_ref.shape[1]), 0)
    for index in range(blk_count):
        chip = source_chip(me >> 1, index // 2, blk_count // 2)
        blk = 2 * chip + ((me & 1) ^ (index % 2))
        load = jnp.int32(0)
        for size, shell in shells:
            load = load + jnp.where(shell == blk, size, 0)
        rows = coef_ref[pl.ds(pl.multiple_of(blk * slot_cap, slot_cap), slot_cap), :]
        ordered[pl.ds(index * slot_cap, slot_cap), :] = jnp.where(count < load, rows, 0.0)
    coef = ordered[...]
    high, low = halves(coef)
    right_ref[...] = jnp.concatenate([high, low, high], axis=0)
    turned = coef.T
    high, low = halves(turned)
    left_ref[...] = jnp.concatenate([high, high, low], axis=1)
    back_ref[...] = jnp.concatenate([high, low], axis=1)
    row = virt_ref[...]
    virt_count = row.shape[1]
    column = jnp.broadcast_to(row, (8, virt_count)).T[:, :1]
    own = energy_ref[owner_ref[me]]
    for stop in range(STOPS):
        both = own + energy_ref[owner_ref[lax.rem(me + blk_count - stop, blk_count)]]
        gap_ref[pl.ds(stop * virt_count, virt_count), :] = 1.0 / ((both - column) - row)


def overlap_kernel(slot_cap, places, *refs):
    *pieces, keep, give, x_high, x_low, total, folded = refs
    first = 1 - (lax.axis_index("blk") & 1)
    here = lax.axis_index("aux")
    for stop in range(STOPS):
        for index, piece in zip(places, pieces):
            high, low = halves(piece[first + stop])
            rows = pl.ds((stop * len(pieces) + index) * slot_cap, slot_cap)
            x_high[rows, :] = high
            x_low[rows, :] = low
    slots = slot_cap * len(pieces)
    own = jnp.concatenate([x_high[:slots, :], x_low[:slots, :]], axis=0)
    both = matmul_nt(own, x_high[...])
    gram = both[:slots] + both[slots:] + matmul_nt(x_high[:slots, :], x_low[...])
    half, band, thin = slots // 2, slots // 4, slots // 8
    for stop in range(1, STOPS):
        square = gram[:, stop * slots : (stop + 1) * slots]
        total[stop - 1] = 2.0 * square - square.T
    square = gram[:, :slots]
    lanes = lax.broadcasted_iota(jnp.int32, (band, slots), 1)
    folded[:band, :] = square[:band]
    folded[band:half, :] = jnp.where(
        lanes < band, pltpu.roll(square[half + band :], band, 1), square[band:half]
    )
    folded[half:, :] = jnp.where(
        lanes[:thin] < half,
        pltpu.roll(square[half + thin : half + band], half, 1),
        square[half : half + thin],
    )
    rest = folded.shape[0] // 2
    for out, part in ((keep, here & 1), (give, 1 - (here & 1))):
        rows = pl.ds(pl.multiple_of(part * half, half), half)
        for stop in range(STOPS - 1):
            out[pl.ds(stop * half, half), :] = total[stop, rows, :]
        out[pl.ds((STOPS - 1) * half, rest), :] = folded[
            pl.ds(pl.multiple_of(part * rest, 8), rest), :
        ]


def density_kernel(steps, *refs):
    parts = len(steps)
    shares = refs[:parts]
    left, right, back, gap, x_high, x_low, out, total, folded, w_high, w_low, density, sems = refs[parts:]
    here = lax.axis_index("aux")
    slots = total.shape[0]
    half = slots // 2
    virt_count = out.shape[0]
    band, rest = slots // 4, folded.shape[0] // 2
    for other in range(2):
        part = here & 1 ^ other
        rows = pl.ds(pl.multiple_of(part * half, half), half)
        share = sum(piece[...] for step, piece in zip(steps, shares) if step & 1 == other)
        for stop in range(1, STOPS):
            total[rows, stop * slots : (stop + 1) * slots] = share[(stop - 1) * half : stop * half]
        folded[pl.ds(pl.multiple_of(part * rest, 8), rest), :] = share[(STOPS - 1) * half :]
    last = folded[half:, :]
    upper = jnp.concatenate(
        [
            folded[:half, :],
            last,
            pltpu.roll(last, half, 1),
            pltpu.roll(folded[band:half, :], slots - band, 1),
        ],
        axis=0,
    )
    row_band = lax.broadcasted_iota(jnp.int32, (slots, slots), 0) // band
    lane_band = lax.broadcasted_iota(jnp.int32, (slots, slots), 1) // band
    total[:, :slots] = jnp.where(lane_band >= row_band, upper, upper.T)
    high, low = halves(total[...])
    half_done = matmul(left[...], jnp.concatenate([high, low, high], axis=0))
    half_done = jnp.concatenate(
        [half_done[:, stop * slots : (stop + 1) * slots] for stop in range(STOPS)], axis=0
    )
    high, low = halves(half_done)
    summed = matmul(jnp.concatenate([high, high, low], axis=1), right[...])
    high, low = halves(summed * gap[...])
    both = matmul(high, back[...])
    weight = both[:, :slots] + both[:, slots:] + matmul(low, back[:, :slots])
    for stop in range(STOPS):
        rows = slice(stop * virt_count, (stop + 1) * virt_count)
        cols = slice(stop * slots, (stop + 1) * slots)
        w_high[:, cols], w_low[:, cols] = halves(weight[rows])
    copies = []
    for index in range(sems.shape[0]):
        band = virt_count // sems.shape[0]
        rows = pl.ds(index * band, band)
        high, low = w_high[rows, :], w_low[rows, :]
        x_all = jnp.concatenate([x_high[...], x_high[...], x_low[...]], axis=0)
        density[rows, :] = matmul(jnp.concatenate([high, low, high], axis=1), x_all)
        copies.append(pltpu.make_async_copy(density.at[rows], out.at[rows], sems.at[index]))
        copies[-1].start()
    for copy in copies:
        copy.wait()


def slots_first(
    occupied_integrals, virtual_coefficients, shell_size, shell_owner, occ_owner, e_occ, e_virt
):
    blk_count = lax.axis_size("blk")
    parts = lax.axis_size("aux")
    _, slot_cap, aux_width = occupied_integrals.shape
    slots, virt_count = virtual_coefficients.shape
    chips = blk_count // 2
    vmem = pl.BlockSpec(memory_space=pltpu.VMEM)
    smem = pl.BlockSpec(memory_space=pltpu.SMEM)
    params = pltpu.CompilerParams(vmem_limit_bytes=24 * 1024 * 1024)

    sent = pl.pallas_call(
        functools.partial(select_kernel, blk_count),
        out_shape=[jax.ShapeDtypeStruct((STOPS + 1, slot_cap, aux_width), F32)] * chips,
        in_specs=[pl.BlockSpec(memory_space=pltpu.HBM)] * 2,
        out_specs=[vmem] * chips,
        scratch_shapes=[
            pltpu.SMEM(occ_owner.shape, jnp.int32),
            pltpu.VMEM(occupied_integrals.shape, F32),
            pltpu.SemaphoreType.DMA,
            pltpu.SemaphoreType.DMA,
        ],
        compiler_params=params,
    )(*[pltpu.with_memory_space_constraint(a, pltpu.HBM) for a in (occ_owner, occupied_integrals)])

    pieces = []
    for step, piece in enumerate(sent):
        if step > 0:
            pairs = [
                (2 * chip + core, 2 * int(partner_chip(chip, step, chips)) + core)
                for chip in range(chips)
                for core in range(2)
            ]
            piece = lax.ppermute(piece, "blk", pairs)
        pieces += [piece, swapped(piece, "blk", 1)]

    left, right, back, gap = pl.pallas_call(
        functools.partial(coefficient_kernel, blk_count),
        out_shape=[
            jax.ShapeDtypeStruct((virt_count, 3 * slots), BF16),
            jax.ShapeDtypeStruct((3 * slots, virt_count), BF16),
            jax.ShapeDtypeStruct((virt_count, 2 * slots), BF16),
            jax.ShapeDtypeStruct((STOPS * virt_count, virt_count), F32),
        ],
        in_specs=[smem] * 4 + [vmem] * 2,
        out_specs=[vmem] * 4,
        scratch_shapes=[pltpu.VMEM((slots, virt_count), F32)],
        compiler_params=params,
    )(
        shell_size,
        shell_owner,
        occ_owner,
        e_occ,
        virtual_coefficients,
        e_virt.reshape(1, virt_count),
    )

    fold = 5 * slots // 8
    places = [2 * step + core for step in reversed(range(chips)) for core in range(2)]
    keep, give, x_high, x_low = pl.pallas_call(
        functools.partial(overlap_kernel, slot_cap, places),
        out_shape=[jax.ShapeDtypeStruct(((STOPS - 1) * slots // 2 + fold // 2, slots), F32)] * 2
        + [jax.ShapeDtypeStruct((STOPS * slots, aux_width), BF16)] * 2,
        in_specs=[vmem] * len(pieces),
        out_specs=[vmem] * 4,
        scratch_shapes=[
            pltpu.VMEM((STOPS - 1, slots, slots), F32),
            pltpu.VMEM((fold, slots), F32),
        ],
        compiler_params=params,
    )(*[pieces[place] for place in places])

    mine = keep + swapped(give, "aux", 1)
    steps = [0, *range(1, parts, 2), *range(2, parts, 2)]
    gathered = [swapped(mine, "aux", step) if step else mine for step in steps]

    bands = 3 if virt_count % 48 == 0 else 1
    density = pl.pallas_call(
        functools.partial(density_kernel, steps),
        out_shape=jax.ShapeDtypeStruct((virt_count, aux_width), F32),
        in_specs=[vmem] * (parts + 6),
        out_specs=pl.BlockSpec(memory_space=pl.ANY),
        scratch_shapes=[
            pltpu.VMEM((slots, STOPS * slots), F32),
            pltpu.VMEM((fold, slots), F32),
            pltpu.VMEM((virt_count, STOPS * slots), BF16),
            pltpu.VMEM((virt_count, STOPS * slots), BF16),
            pltpu.VMEM((virt_count, aux_width), F32),
            pltpu.SemaphoreType.DMA((bands,)),
        ],
        compiler_params=params,
    )(*gathered, left, right, back, gap, x_high, x_low)
    return density.reshape(1, virt_count, aux_width)


def per_device(occupied_integrals, virtual_coefficients, *rest):
    blk_count = lax.axis_size("blk")
    slots, virt_count = virtual_coefficients.shape
    paired = blk_count % 2 == 0 and blk_count == occupied_integrals.shape[0]
    parts = lax.axis_size("aux")
    shared = parts > 1 and parts & (parts - 1) == 0 and slots % 128 == 0 and slots <= virt_count
    run = slots_first if paired and shared else transformed_first
    return run(occupied_integrals, virtual_coefficients, *rest)


def solution(mesh):
    in_specs = (P(None, "blk", "aux"), P(), P(), P(), P(), P(), P())
    out_specs = P("blk", None, "aux")
    return jax.shard_map(
        per_device, mesh=mesh, in_specs=in_specs, out_specs=out_specs, check_vma=False
    )
```

```python
import functools

import jax
import jax.numpy as jnp
from jax import lax
from jax.experimental import pallas as pl
from jax.experimental.pallas import tpu as pltpu
from jax.sharding import PartitionSpec as P

STOPS = 3
BF16 = jnp.bfloat16
F32 = jnp.float32


def shifted(value, axis, steps):
    count = lax.axis_size(axis)
    pairs = [(source, (source + steps) % count) for source in range(count)]
    return lax.ppermute(value, axis, pairs)


def swapped(value, axis, step):
    return lax.ppermute(value, axis, [(i, i ^ step) for i in range(lax.axis_size(axis))])


def live_slots(shell_size, shell_owner, blk_count, slot_cap):
    owner_hits = (shell_owner[:, None] == jnp.arange(blk_count, dtype=jnp.int32)[None, :]).astype(
        jnp.int32
    )
    slot_load = jnp.sum(shell_size[:, None] * owner_hits, axis=0)
    return (jnp.arange(slot_cap, dtype=jnp.int32)[None, :] < slot_load[:, None]).astype(F32)


def transformed_first(
    occupied_integrals, virtual_coefficients, shell_size, shell_owner, occ_owner, e_occ, e_virt
):
    blk_count = lax.axis_size("blk")
    occ_total = occupied_integrals.shape[0]
    slot_cap = occupied_integrals.shape[1]
    aux_width = occupied_integrals.shape[2]
    virt_count = virtual_coefficients.shape[1]
    occ_local = occ_total // blk_count
    pair_rows = occ_local * virt_count
    highest = lax.Precision.HIGHEST
    live_mask = live_slots(shell_size, shell_owner, blk_count, slot_cap)
    masked_coef = (
        virtual_coefficients.reshape(blk_count, slot_cap, virt_count) * live_mask[:, :, None]
    )
    grouped = jnp.take(occupied_integrals, occ_owner, axis=0).reshape(
        blk_count, occ_local, slot_cap, aux_width
    )
    owned = jnp.einsum(
        "dnkq,dkv->nvq",
        lax.all_to_all(grouped, "blk", split_axis=0, concat_axis=0, tiled=True),
        masked_coef,
        precision=highest,
    )
    own_block = owned.reshape(pair_rows, aux_width)
    my_index = lax.axis_index("blk")
    block_energy = jnp.take(e_occ, occ_owner).reshape(blk_count, occ_local)
    own_energy = lax.dynamic_index_in_dim(block_energy, my_index, 0, keepdims=False)
    partners = [own_block]
    partner_energies = [own_energy]
    passing = own_block
    for stop in range(1, STOPS):
        passing = shifted(passing, "blk", 1)
        partners.append(passing)
        partner_index = jnp.mod(my_index - stop, blk_count)
        partner_energies.append(
            lax.dynamic_index_in_dim(block_energy, partner_index, 0, keepdims=False)
        )
    density = jnp.zeros((pair_rows, aux_width), F32)
    for stop in range(STOPS):
        pair_ints = jnp.einsum("rq,cq->rc", own_block, partners[stop], precision=highest)
        pair_ints = pair_ints.reshape(occ_local, virt_count, occ_local, virt_count)
        summed = lax.psum(2.0 * pair_ints - pair_ints.transpose(0, 3, 2, 1), "aux")
        amplitudes = (
            summed
            / (
                own_energy[:, None, None, None]
                + partner_energies[stop][None, None, :, None]
                - e_virt[None, :, None, None]
                - e_virt[None, None, None, :]
            )
        ).reshape(pair_rows, pair_rows)
        density = density + jnp.dot(amplitudes, partners[stop], precision=highest)
    return density.reshape(occ_local, virt_count, aux_width)


def halves(value):
    high = value.astype(BF16)
    return high, (value - high.astype(F32)).astype(BF16)


def matmul(a, b):
    return jnp.dot(a, b, preferred_element_type=F32)


def matmul_nt(a, b):
    return lax.dot_general(a, b, (((1,), (1,)), ((), ())), preferred_element_type=F32)


def partner_chip(chip, step, chips):
    return chip ^ step if chips & (chips - 1) == 0 else lax.rem(chip + step, chips)


def source_chip(chip, step, chips):
    return chip ^ step if chips & (chips - 1) == 0 else lax.rem(chip + chips - step, chips)


def select_kernel(blk_count, owner_hbm, x_hbm, *refs):
    *outs, owner_ref, x_ref, owner_sem, x_sem = refs
    chips = blk_count // 2
    my_chip = lax.axis_index("blk") >> 1
    reads = [
        pltpu.make_async_copy(owner_hbm, owner_ref, owner_sem),
        pltpu.make_async_copy(x_hbm, x_ref, x_sem),
    ]
    for read in reads:
        read.start()
    for read in reads:
        read.wait()
    for step, out in enumerate(outs):
        last = 2 * partner_chip(my_chip, step, chips) + 1
        for stop in range(STOPS + 1):
            out[stop] = x_ref[owner_ref[lax.rem(last + blk_count - stop, blk_count)]]


def coefficient_kernel(
    blk_count,
    size_ref,
    shell_ref,
    owner_ref,
    energy_ref,
    coef_ref,
    virt_ref,
    left_ref,
    right_ref,
    back_ref,
    gap_ref,
    ordered,
):
    slots = coef_ref.shape[0]
    slot_cap = slots // blk_count
    me = lax.axis_index("blk")
    shells = [(size_ref[s], shell_ref[s]) for s in range(size_ref.shape[0])]
    count = lax.broadcasted_iota(jnp.int32, (slot_cap, coef_ref.shape[1]), 0)
    for index in range(blk_count):
        chip = source_chip(me >> 1, index // 2, blk_count // 2)
        blk = 2 * chip + ((me & 1) ^ (index % 2))
        load = jnp.int32(0)
        for size, shell in shells:
            load = load + jnp.where(shell == blk, size, 0)
        rows = coef_ref[pl.ds(pl.multiple_of(blk * slot_cap, slot_cap), slot_cap), :]
        ordered[pl.ds(index * slot_cap, slot_cap), :] = jnp.where(count < load, rows, 0.0)
    coef = ordered[...]
    high, low = halves(coef)
    right_ref[...] = jnp.concatenate([high, low, high], axis=0)
    turned = coef.T
    high, low = halves(turned)
    left_ref[...] = jnp.concatenate([high, high, low], axis=1)
    back_ref[...] = jnp.concatenate([high, low], axis=1)
    row = virt_ref[...]
    virt_count = row.shape[1]
    column = jnp.broadcast_to(row, (8, virt_count)).T[:, :1]
    own = energy_ref[owner_ref[me]]
    for stop in range(STOPS):
        both = own + energy_ref[owner_ref[lax.rem(me + blk_count - stop, blk_count)]]
        gap_ref[pl.ds(stop * virt_count, virt_count), :] = 1.0 / ((both - column) - row)


def overlap_kernel(slot_cap, places, *refs):
    *pieces, keep, give, x_high, x_low, total, folded = refs
    first = 1 - (lax.axis_index("blk") & 1)
    here = lax.axis_index("aux")
    for stop in range(STOPS):
        for index, piece in zip(places, pieces):
            high, low = halves(piece[first + stop])
            rows = pl.ds((stop * len(pieces) + index) * slot_cap, slot_cap)
            x_high[rows, :] = high
            x_low[rows, :] = low
    slots = slot_cap * len(pieces)
    own = jnp.concatenate([x_high[:slots, :], x_low[:slots, :]], axis=0)
    both = matmul_nt(own, x_high[...])
    gram = both[:slots] + both[slots:] + matmul_nt(x_high[:slots, :], x_low[...])
    half, band, thin = slots // 2, slots // 4, slots // 8
    for stop in range(1, STOPS):
        square = gram[:, stop * slots : (stop + 1) * slots]
        total[stop - 1] = 2.0 * square - square.T
    square = gram[:, :slots]
    lanes = lax.broadcasted_iota(jnp.int32, (band, slots), 1)
    folded[:band, :] = square[:band]
    folded[band:half, :] = jnp.where(
        lanes < band, pltpu.roll(square[half + band :], band, 1), square[band:half]
    )
    folded[half:, :] = jnp.where(
        lanes[:thin] < half,
        pltpu.roll(square[half + thin : half + band], half, 1),
        square[half : half + thin],
    )
    rest = folded.shape[0] // 2
    for out, part in ((keep, here & 1), (give, 1 - (here & 1))):
        packed = folded[pl.ds(pl.multiple_of(part * rest, 8), rest), :]
        out[...] = jnp.concatenate([total[part], packed], axis=0)


def weigh(total, left, right, back, gap, w_high, w_low):
    slots = total.shape[0]
    virt_count = w_high.shape[0]
    stops = total.shape[1] // slots
    high, low = halves(total)
    half_done = matmul(left[...], jnp.concatenate([high, low, high], axis=0))
    half_done = jnp.concatenate(
        [half_done[:, stop * slots : (stop + 1) * slots] for stop in range(stops)], axis=0
    )
    high, low = halves(half_done)
    summed = matmul(jnp.concatenate([high, high, low], axis=1), right[...])
    high, low = halves(summed * gap)
    both = matmul(high, back[...])
    weight = both[:, :slots] + both[:, slots:] + matmul(low, back[:, :slots])
    for stop in range(stops):
        cols = slice(stop * slots, (stop + 1) * slots)
        w_high[:, cols], w_low[:, cols] = halves(
            weight[stop * virt_count : (stop + 1) * virt_count]
        )


def rows_of(ref, stop, count):
    return ref[pl.ds(pl.multiple_of(stop * count, count), count), :]


def first_density_kernel(*refs):
    *shares, left, right, back, gap, x_high, x_low, out, w_high, w_low = refs
    slots = left.shape[1] // 3
    stop = 1 + (lax.axis_index("aux") & 1)
    square = sum(piece[:slots, :] for piece in shares)
    weigh(square, left, right, back, rows_of(gap, stop, out.shape[0]), w_high, w_low)
    high, low = rows_of(x_high, stop, slots), rows_of(x_low, stop, slots)
    x_all = jnp.concatenate([high, high, low], axis=0)
    out[...] = matmul(jnp.concatenate([w_high[...], w_low[...], w_high[...]], axis=1), x_all)


def last_density_kernel(count, *refs):
    first, second = refs[:count], refs[count : 2 * count]
    before, left, right, back, gap, x_high, x_low, out, *scratch = refs[2 * count :]
    total, folded, w_high, w_low, density, sems = scratch
    mine = lax.axis_index("aux") & 1
    stop = 2 - mine
    slots = total.shape[0]
    half = slots // 2
    band, rest = slots // 4, folded.shape[0] // 2
    virt_count = out.shape[0]
    for part, pieces in ((mine, first), (1 - mine, second)):
        folded[pl.ds(pl.multiple_of(part * rest, 8), rest), :] = sum(
            piece[slots:, :] for piece in pieces
        )
    total[:, slots:] = sum(piece[:slots, :] for piece in second)
    last = folded[half:, :]
    upper = jnp.concatenate(
        [
            folded[:half, :],
            last,
            pltpu.roll(last, half, 1),
            pltpu.roll(folded[band:half, :], slots - band, 1),
        ],
        axis=0,
    )
    row_band = lax.broadcasted_iota(jnp.int32, (slots, slots), 0) // band
    lane_band = lax.broadcasted_iota(jnp.int32, (slots, slots), 1) // band
    total[:, :slots] = jnp.where(lane_band >= row_band, upper, upper.T)
    gaps = jnp.concatenate([gap[:virt_count, :], rows_of(gap, stop, virt_count)], axis=0)
    weigh(total[...], left, right, back, gaps, w_high, w_low)
    x_high = jnp.concatenate([x_high[:slots, :], rows_of(x_high, stop, slots)], axis=0)
    x_low = jnp.concatenate([x_low[:slots, :], rows_of(x_low, stop, slots)], axis=0)
    copies = []
    for index in range(sems.shape[0]):
        band = virt_count // sems.shape[0]
        rows = pl.ds(index * band, band)
        high, low = w_high[rows, :], w_low[rows, :]
        both = matmul(jnp.concatenate([high, low], axis=0), x_high)
        density[rows, :] = before[rows, :] + both[:band] + both[band:] + matmul(high, x_low)
        copies.append(pltpu.make_async_copy(density.at[rows], out.at[rows], sems.at[index]))
        copies[-1].start()
    for copy in copies:
        copy.wait()


def slots_first(
    occupied_integrals, virtual_coefficients, shell_size, shell_owner, occ_owner, e_occ, e_virt
):
    blk_count = lax.axis_size("blk")
    parts = lax.axis_size("aux")
    _, slot_cap, aux_width = occupied_integrals.shape
    slots, virt_count = virtual_coefficients.shape
    chips = blk_count // 2
    vmem = pl.BlockSpec(memory_space=pltpu.VMEM)
    smem = pl.BlockSpec(memory_space=pltpu.SMEM)
    params = pltpu.CompilerParams(vmem_limit_bytes=24 * 1024 * 1024)

    sent = pl.pallas_call(
        functools.partial(select_kernel, blk_count),
        out_shape=[jax.ShapeDtypeStruct((STOPS + 1, slot_cap, aux_width), F32)] * chips,
        in_specs=[pl.BlockSpec(memory_space=pltpu.HBM)] * 2,
        out_specs=[vmem] * chips,
        scratch_shapes=[
            pltpu.SMEM(occ_owner.shape, jnp.int32),
            pltpu.VMEM(occupied_integrals.shape, F32),
            pltpu.SemaphoreType.DMA,
            pltpu.SemaphoreType.DMA,
        ],
        compiler_params=params,
    )(*[pltpu.with_memory_space_constraint(a, pltpu.HBM) for a in (occ_owner, occupied_integrals)])

    pieces = []
    for step, piece in enumerate(sent):
        if step > 0:
            pairs = [
                (2 * chip + core, 2 * int(partner_chip(chip, step, chips)) + core)
                for chip in range(chips)
                for core in range(2)
            ]
            piece = lax.ppermute(piece, "blk", pairs)
        pieces += [piece, swapped(piece, "blk", 1)]

    left, right, back, gap = pl.pallas_call(
        functools.partial(coefficient_kernel, blk_count),
        out_shape=[
            jax.ShapeDtypeStruct((virt_count, 3 * slots), BF16),
            jax.ShapeDtypeStruct((3 * slots, virt_count), BF16),
            jax.ShapeDtypeStruct((virt_count, 2 * slots), BF16),
            jax.ShapeDtypeStruct((STOPS * virt_count, virt_count), F32),
        ],
        in_specs=[smem] * 4 + [vmem] * 2,
        out_specs=[vmem] * 4,
        scratch_shapes=[pltpu.VMEM((slots, virt_count), F32)],
        compiler_params=params,
    )(
        shell_size,
        shell_owner,
        occ_owner,
        e_occ,
        virtual_coefficients,
        e_virt.reshape(1, virt_count),
    )

    fold = 5 * slots // 8
    places = [2 * step + core for step in reversed(range(chips)) for core in range(2)]
    keep, give, x_high, x_low = pl.pallas_call(
        functools.partial(overlap_kernel, slot_cap, places),
        out_shape=[jax.ShapeDtypeStruct((slots + fold // 2, slots), F32)] * 2
        + [jax.ShapeDtypeStruct((STOPS * slots, aux_width), BF16)] * 2,
        in_specs=[vmem] * len(pieces),
        out_specs=[vmem] * 4,
        scratch_shapes=[
            pltpu.VMEM((STOPS - 1, slots, slots), F32),
            pltpu.VMEM((fold, slots), F32),
        ],
        compiler_params=params,
    )(*[pieces[place] for place in places])

    taken = swapped(give, "aux", 1)
    mine = keep + taken
    mine, left = lax.optimization_barrier((mine, left))
    evens = [mine] + [swapped(mine, "aux", step) for step in range(2, parts, 2)]
    held = mine
    odds = [swapped(held, "aux", step) for step in range(1, parts, 2)]
    bands = 3 if virt_count % 48 == 0 else 1
    flops = 18 * virt_count * slots * (slots + 2 * virt_count + aux_width)

    first = pl.pallas_call(
        first_density_kernel,
        out_shape=jax.ShapeDtypeStruct((virt_count, aux_width), F32),
        in_specs=[vmem] * (len(evens) + 6),
        out_specs=vmem,
        scratch_shapes=[pltpu.VMEM((virt_count, slots), BF16)] * 2,
        compiler_params=params,
        cost_estimate=pl.CostEstimate(flops=flops, bytes_accessed=0, transcendentals=0),
    )(*evens, left, right, back, gap, x_high, x_low)
    density = pl.pallas_call(
        functools.partial(last_density_kernel, len(evens)),
        out_shape=jax.ShapeDtypeStruct((virt_count, aux_width), F32),
        in_specs=[vmem] * (len(evens) + len(odds) + 7),
        out_specs=pl.BlockSpec(memory_space=pl.ANY),
        scratch_shapes=[
            pltpu.VMEM((slots, 2 * slots), F32),
            pltpu.VMEM((fold, slots), F32),
            pltpu.VMEM((virt_count, 2 * slots), BF16),
            pltpu.VMEM((virt_count, 2 * slots), BF16),
            pltpu.VMEM((virt_count, aux_width), F32),
            pltpu.SemaphoreType.DMA((bands,)),
        ],
        compiler_params=params,
    )(*evens, *odds, first, left, right, back, gap, x_high, x_low)
    return density.reshape(1, virt_count, aux_width)


def per_device(occupied_integrals, virtual_coefficients, *rest):
    blk_count = lax.axis_size("blk")
    slots, virt_count = virtual_coefficients.shape
    paired = blk_count % 2 == 0 and blk_count == occupied_integrals.shape[0]
    parts = lax.axis_size("aux")
    shared = parts > 1 and parts & (parts - 1) == 0 and slots % 128 == 0 and slots <= virt_count
    run = slots_first if paired and shared else transformed_first
    return run(occupied_integrals, virtual_coefficients, *rest)


def solution(mesh):
    in_specs = (P(None, "blk", "aux"), P(), P(), P(), P(), P(), P())
    out_specs = P("blk", None, "aux")
    return jax.shard_map(
        per_device, mesh=mesh, in_specs=in_specs, out_specs=out_specs, check_vma=False
    )
```

```python
import functools

import jax
import jax.numpy as jnp
from jax import lax
from jax.experimental import pallas as pl
from jax.experimental.pallas import tpu as pltpu
from jax.sharding import PartitionSpec as P

STOPS = 3
BF16 = jnp.bfloat16
F32 = jnp.float32


def shifted(value, axis, steps):
    count = lax.axis_size(axis)
    pairs = [(source, (source + steps) % count) for source in range(count)]
    return lax.ppermute(value, axis, pairs)


def swapped(value, axis, step):
    return lax.ppermute(value, axis, [(i, i ^ step) for i in range(lax.axis_size(axis))])


def live_slots(shell_size, shell_owner, blk_count, slot_cap):
    owner_hits = (shell_owner[:, None] == jnp.arange(blk_count, dtype=jnp.int32)[None, :]).astype(
        jnp.int32
    )
    slot_load = jnp.sum(shell_size[:, None] * owner_hits, axis=0)
    return (jnp.arange(slot_cap, dtype=jnp.int32)[None, :] < slot_load[:, None]).astype(F32)


def transformed_first(
    occupied_integrals, virtual_coefficients, shell_size, shell_owner, occ_owner, e_occ, e_virt
):
    blk_count = lax.axis_size("blk")
    occ_total = occupied_integrals.shape[0]
    slot_cap = occupied_integrals.shape[1]
    aux_width = occupied_integrals.shape[2]
    virt_count = virtual_coefficients.shape[1]
    occ_local = occ_total // blk_count
    pair_rows = occ_local * virt_count
    highest = lax.Precision.HIGHEST
    live_mask = live_slots(shell_size, shell_owner, blk_count, slot_cap)
    masked_coef = (
        virtual_coefficients.reshape(blk_count, slot_cap, virt_count) * live_mask[:, :, None]
    )
    grouped = jnp.take(occupied_integrals, occ_owner, axis=0).reshape(
        blk_count, occ_local, slot_cap, aux_width
    )
    owned = jnp.einsum(
        "dnkq,dkv->nvq",
        lax.all_to_all(grouped, "blk", split_axis=0, concat_axis=0, tiled=True),
        masked_coef,
        precision=highest,
    )
    own_block = owned.reshape(pair_rows, aux_width)
    my_index = lax.axis_index("blk")
    block_energy = jnp.take(e_occ, occ_owner).reshape(blk_count, occ_local)
    own_energy = lax.dynamic_index_in_dim(block_energy, my_index, 0, keepdims=False)
    partners = [own_block]
    partner_energies = [own_energy]
    passing = own_block
    for stop in range(1, STOPS):
        passing = shifted(passing, "blk", 1)
        partners.append(passing)
        partner_index = jnp.mod(my_index - stop, blk_count)
        partner_energies.append(
            lax.dynamic_index_in_dim(block_energy, partner_index, 0, keepdims=False)
        )
    density = jnp.zeros((pair_rows, aux_width), F32)
    for stop in range(STOPS):
        pair_ints = jnp.einsum("rq,cq->rc", own_block, partners[stop], precision=highest)
        pair_ints = pair_ints.reshape(occ_local, virt_count, occ_local, virt_count)
        summed = lax.psum(2.0 * pair_ints - pair_ints.transpose(0, 3, 2, 1), "aux")
        amplitudes = (
            summed
            / (
                own_energy[:, None, None, None]
                + partner_energies[stop][None, None, :, None]
                - e_virt[None, :, None, None]
                - e_virt[None, None, None, :]
            )
        ).reshape(pair_rows, pair_rows)
        density = density + jnp.dot(amplitudes, partners[stop], precision=highest)
    return density.reshape(occ_local, virt_count, aux_width)


def halves(value):
    high = value.astype(BF16)
    return high, (value - high.astype(F32)).astype(BF16)


def matmul(a, b):
    return jnp.dot(a, b, preferred_element_type=F32)


def matmul_nt(a, b):
    return lax.dot_general(a, b, (((1,), (1,)), ((), ())), preferred_element_type=F32)


def partner_chip(chip, step, chips):
    return chip ^ step if chips & (chips - 1) == 0 else lax.rem(chip + step, chips)


def source_chip(chip, step, chips):
    return chip ^ step if chips & (chips - 1) == 0 else lax.rem(chip + chips - step, chips)


def select_kernel(blk_count, owner_hbm, x_hbm, *refs):
    *outs, owner_ref, x_ref, owner_sem, x_sem = refs
    chips = blk_count // 2
    me = lax.axis_index("blk")
    my_chip, my_core = me >> 1, me & 1
    reads = [
        pltpu.make_async_copy(owner_hbm, owner_ref, owner_sem),
        pltpu.make_async_copy(x_hbm, x_ref, x_sem),
    ]
    for read in reads:
        read.start()
    for read in reads:
        read.wait()

    def rows(block):
        return x_ref[owner_ref[lax.rem(block + blk_count, blk_count)]]

    for step in range(chips):
        last = 2 * partner_chip(my_chip, step, chips)
        mine, theirs = last - 2 + 3 * my_core, last - 2 + 3 * (1 - my_core)
        whole = outs[2 * step]
        whole[0], whole[1] = rows(last), rows(last - 1)
        if step == chips - 1:
            whole[2], whole[3] = rows(last + 1), rows(last - 2)
            continue
        whole[2] = rows(mine)
        rest = outs[2 * step + 1]
        if step == 0:
            rest[0], rest[1] = whole[0], whole[1]
        rest[rest.shape[0] - 1] = rows(theirs)


def coefficient_kernel(
    blk_count,
    size_ref,
    shell_ref,
    owner_ref,
    energy_ref,
    coef_ref,
    virt_ref,
    left_ref,
    right_ref,
    back_ref,
    gap_ref,
    ordered,
):
    slots = coef_ref.shape[0]
    slot_cap = slots // blk_count
    me = lax.axis_index("blk")
    shells = [(size_ref[s], shell_ref[s]) for s in range(size_ref.shape[0])]
    count = lax.broadcasted_iota(jnp.int32, (slot_cap, coef_ref.shape[1]), 0)
    for index in range(blk_count):
        chip = source_chip(me >> 1, index // 2, blk_count // 2)
        blk = 2 * chip + ((me & 1) ^ (index % 2))
        load = jnp.int32(0)
        for size, shell in shells:
            load = load + jnp.where(shell == blk, size, 0)
        rows = coef_ref[pl.ds(pl.multiple_of(blk * slot_cap, slot_cap), slot_cap), :]
        ordered[pl.ds(index * slot_cap, slot_cap), :] = jnp.where(count < load, rows, 0.0)
    coef = ordered[...]
    high, low = halves(coef)
    right_ref[...] = jnp.concatenate([high, low, high], axis=0)
    turned = coef.T
    high, low = halves(turned)
    left_ref[...] = jnp.concatenate([high, high, low], axis=1)
    back_ref[...] = jnp.concatenate([high, low], axis=1)
    row = virt_ref[...]
    virt_count = row.shape[1]
    column = jnp.broadcast_to(row, (8, virt_count)).T[:, :1]
    own = energy_ref[owner_ref[me]]
    for stop in range(STOPS):
        both = own + energy_ref[owner_ref[lax.rem(me + blk_count - stop, blk_count)]]
        gap_ref[pl.ds(stop * virt_count, virt_count), :] = 1.0 / ((both - column) - row)


def join_kernel(*refs):
    *pieces, out = refs
    for index, piece in enumerate(pieces):
        out[index] = piece[0]


def overlap_kernel(slot_cap, layout, *refs):
    *operands, keep, give, x_high, x_low, total, folded = refs
    count = 1 + max(place for entries in layout for _, _, place in entries)
    my_core = lax.axis_index("blk") & 1
    here = lax.axis_index("aux")
    for entries, operand in zip(layout, operands):
        for row, offset, place in entries:
            stop = lax.rem(offset + my_core, STOPS)
            high, low = halves(operand[3 - my_core if row == 3 else row])
            target = pl.ds(pl.multiple_of((stop * count + place) * slot_cap, slot_cap), slot_cap)
            x_high[target, :] = high
            x_low[target, :] = low
    slots = slot_cap * count
    own = jnp.concatenate([x_high[:slots, :], x_low[:slots, :]], axis=0)
    both = matmul_nt(own, x_high[...])
    gram = both[:slots] + both[slots:] + matmul_nt(x_high[:slots, :], x_low[...])
    half, band, thin = slots // 2, slots // 4, slots // 8
    for stop in range(1, STOPS):
        square = gram[:, stop * slots : (stop + 1) * slots]
        total[stop - 1] = 2.0 * square - square.T
    square = gram[:, :slots]
    lanes = lax.broadcasted_iota(jnp.int32, (band, slots), 1)
    folded[:band, :] = square[:band]
    folded[band:half, :] = jnp.where(
        lanes < band, pltpu.roll(square[half + band :], band, 1), square[band:half]
    )
    folded[half:, :] = jnp.where(
        lanes[:thin] < half,
        pltpu.roll(square[half + thin : half + band], half, 1),
        square[half : half + thin],
    )
    rest = folded.shape[0] // 2
    for out, part in ((keep, here & 1), (give, 1 - (here & 1))):
        packed = folded[pl.ds(pl.multiple_of(part * rest, 8), rest), :]
        out[...] = jnp.concatenate([total[part], packed], axis=0)


def weigh(total, left, right, back, gap, w_high, w_low):
    slots = total.shape[0]
    virt_count = w_high.shape[0]
    stops = total.shape[1] // slots
    high, low = halves(total)
    half_done = matmul(left[...], jnp.concatenate([high, low, high], axis=0))
    half_done = jnp.concatenate(
        [half_done[:, stop * slots : (stop + 1) * slots] for stop in range(stops)], axis=0
    )
    high, low = halves(half_done)
    summed = matmul(jnp.concatenate([high, high, low], axis=1), right[...])
    high, low = halves(summed * gap)
    both = matmul(high, back[...])
    weight = both[:, :slots] + both[:, slots:] + matmul(low, back[:, :slots])
    for stop in range(stops):
        cols = slice(stop * slots, (stop + 1) * slots)
        w_high[:, cols], w_low[:, cols] = halves(
            weight[stop * virt_count : (stop + 1) * virt_count]
        )


def rows_of(ref, stop, count):
    return ref[pl.ds(pl.multiple_of(stop * count, count), count), :]


def first_density_kernel(*refs):
    *shares, left, right, back, gap, x_high, x_low, out, w_high, w_low = refs
    slots = left.shape[1] // 3
    stop = 1 + (lax.axis_index("aux") & 1)
    square = sum(piece[:slots, :] for piece in shares)
    weigh(square, left, right, back, rows_of(gap, stop, out.shape[0]), w_high, w_low)
    high, low = rows_of(x_high, stop, slots), rows_of(x_low, stop, slots)
    x_all = jnp.concatenate([high, high, low], axis=0)
    out[...] = matmul(jnp.concatenate([w_high[...], w_low[...], w_high[...]], axis=1), x_all)


def last_density_kernel(count, *refs):
    first, second = refs[:count], refs[count : 2 * count]
    before, left, right, back, gap, x_high, x_low, out, *scratch = refs[2 * count :]
    total, folded, w_high, w_low, density, sems = scratch
    mine = lax.axis_index("aux") & 1
    stop = 2 - mine
    slots = total.shape[0]
    half = slots // 2
    band, rest = slots // 4, folded.shape[0] // 2
    virt_count = out.shape[0]
    for part, pieces in ((mine, first), (1 - mine, second)):
        folded[pl.ds(pl.multiple_of(part * rest, 8), rest), :] = sum(
            piece[slots:, :] for piece in pieces
        )
    total[:, slots:] = sum(piece[:slots, :] for piece in second)
    last = folded[half:, :]
    upper = jnp.concatenate(
        [
            folded[:half, :],
            last,
            pltpu.roll(last, half, 1),
            pltpu.roll(folded[band:half, :], slots - band, 1),
        ],
        axis=0,
    )
    row_band = lax.broadcasted_iota(jnp.int32, (slots, slots), 0) // band
    lane_band = lax.broadcasted_iota(jnp.int32, (slots, slots), 1) // band
    total[:, :slots] = jnp.where(lane_band >= row_band, upper, upper.T)
    gaps = jnp.concatenate([gap[:virt_count, :], rows_of(gap, stop, virt_count)], axis=0)
    weigh(total[...], left, right, back, gaps, w_high, w_low)
    x_high = jnp.concatenate([x_high[:slots, :], rows_of(x_high, stop, slots)], axis=0)
    x_low = jnp.concatenate([x_low[:slots, :], rows_of(x_low, stop, slots)], axis=0)
    copies = []
    for index in range(sems.shape[0]):
        band = virt_count // sems.shape[0]
        rows = pl.ds(index * band, band)
        high, low = w_high[rows, :], w_low[rows, :]
        both = matmul(jnp.concatenate([high, low], axis=0), x_high)
        density[rows, :] = before[rows, :] + both[:band] + both[band:] + matmul(high, x_low)
        copies.append(pltpu.make_async_copy(density.at[rows], out.at[rows], sems.at[index]))
        copies[-1].start()
    for copy in copies:
        copy.wait()


def slots_first(
    occupied_integrals, virtual_coefficients, shell_size, shell_owner, occ_owner, e_occ, e_virt
):
    blk_count = lax.axis_size("blk")
    parts = lax.axis_size("aux")
    _, slot_cap, aux_width = occupied_integrals.shape
    slots, virt_count = virtual_coefficients.shape
    chips = blk_count // 2
    vmem = pl.BlockSpec(memory_space=pltpu.VMEM)
    smem = pl.BlockSpec(memory_space=pltpu.SMEM)
    params = pltpu.CompilerParams(vmem_limit_bytes=24 * 1024 * 1024)

    def block(count):
        return jax.ShapeDtypeStruct((count, slot_cap, aux_width), F32)

    sent = pl.pallas_call(
        functools.partial(select_kernel, blk_count),
        out_shape=[block(STOPS)] * 2 + [block(STOPS), block(1)] * (chips - 2) + [block(4)],
        in_specs=[pl.BlockSpec(memory_space=pltpu.HBM)] * 2,
        out_specs=[vmem] * (2 * chips - 1),
        scratch_shapes=[
            pltpu.SMEM(occ_owner.shape, jnp.int32),
            pltpu.VMEM(occupied_integrals.shape, F32),
            pltpu.SemaphoreType.DMA,
            pltpu.SemaphoreType.DMA,
        ],
        compiler_params=params,
    )(*[pltpu.with_memory_space_constraint(a, pltpu.HBM) for a in (occ_owner, occupied_integrals)])

    def entries(place, rows=STOPS):
        return [(row, row, place) for row in range(rows)]

    own = [(sent[0], entries(0)), (swapped(sent[1], "blk", 1), entries(1))]
    whole, rest = [], []
    for step in range(1, chips):
        ways = [
            [
                (2 * chip + core, 2 * int(partner_chip(chip, step, chips)) + (core ^ cross))
                for chip in range(chips)
                for core in range(2)
            ]
            for cross in range(2)
        ]
        piece = lax.ppermute(sent[2 * step], "blk", ways[0])
        if step == chips - 1:
            both = [[*entries(place, 2), (3, 2, place)] for place in (2 * step, 2 * step + 1)]
            held, sibling = lax.optimization_barrier((piece, own[1][0]))
            own[1] = (sibling, own[1][1])
            whole += [(piece, both[0]), (swapped(held, "blk", 1), both[1])]
            continue
        other = lax.ppermute(sent[2 * step + 1], "blk", ways[1])
        whole.append((piece, entries(2 * step)))
        whole.append((swapped(piece, "blk", 1), entries(2 * step + 1, 2)))
        rest.append(other)
    joined = pl.pallas_call(
        join_kernel,
        out_shape=block(chips - 2),
        in_specs=[vmem] * (chips - 2),
        out_specs=vmem,
        compiler_params=params,
        cost_estimate=pl.CostEstimate(flops=2 * 10**9, bytes_accessed=0, transcendentals=0),
    )(*rest)
    last = [(joined, [(row, 2, 2 * step + 1) for row, step in enumerate(range(1, chips - 1))])]
    pieces = whole[4:6] + whole[2:4] + whole[:2] + own + last
    operands, layout = zip(*pieces)

    left, right, back, gap = pl.pallas_call(
        functools.partial(coefficient_kernel, blk_count),
        out_shape=[
            jax.ShapeDtypeStruct((virt_count, 3 * slots), BF16),
            jax.ShapeDtypeStruct((3 * slots, virt_count), BF16),
            jax.ShapeDtypeStruct((virt_count, 2 * slots), BF16),
            jax.ShapeDtypeStruct((STOPS * virt_count, virt_count), F32),
        ],
        in_specs=[smem] * 4 + [vmem] * 2,
        out_specs=[vmem] * 4,
        scratch_shapes=[pltpu.VMEM((slots, virt_count), F32)],
        compiler_params=params,
    )(
        shell_size,
        shell_owner,
        occ_owner,
        e_occ,
        virtual_coefficients,
        e_virt.reshape(1, virt_count),
    )

    fold = 5 * slots // 8
    keep, give, x_high, x_low = pl.pallas_call(
        functools.partial(overlap_kernel, slot_cap, layout),
        out_shape=[jax.ShapeDtypeStruct((slots + fold // 2, slots), F32)] * 2
        + [jax.ShapeDtypeStruct((STOPS * slots, aux_width), BF16)] * 2,
        in_specs=[vmem] * len(operands),
        out_specs=[vmem] * 4,
        scratch_shapes=[
            pltpu.VMEM((STOPS - 1, slots, slots), F32),
            pltpu.VMEM((fold, slots), F32),
        ],
        compiler_params=params,
    )(*operands)

    taken = swapped(give, "aux", 1)
    mine = keep + taken
    mine, left = lax.optimization_barrier((mine, left))
    evens = [mine] + [swapped(mine, "aux", step) for step in range(2, parts, 2)]
    held = mine
    odds = [swapped(held, "aux", step) for step in range(1, parts, 2)]
    bands = 3 if virt_count % 48 == 0 else 1
    flops = 18 * virt_count * slots * (slots + 2 * virt_count + aux_width)

    first = pl.pallas_call(
        first_density_kernel,
        out_shape=jax.ShapeDtypeStruct((virt_count, aux_width), F32),
        in_specs=[vmem] * (len(evens) + 6),
        out_specs=vmem,
        scratch_shapes=[pltpu.VMEM((virt_count, slots), BF16)] * 2,
        compiler_params=params,
        cost_estimate=pl.CostEstimate(flops=flops, bytes_accessed=0, transcendentals=0),
    )(*evens, left, right, back, gap, x_high, x_low)
    density = pl.pallas_call(
        functools.partial(last_density_kernel, len(evens)),
        out_shape=jax.ShapeDtypeStruct((virt_count, aux_width), F32),
        in_specs=[vmem] * (len(evens) + len(odds) + 7),
        out_specs=pl.BlockSpec(memory_space=pl.ANY),
        scratch_shapes=[
            pltpu.VMEM((slots, 2 * slots), F32),
            pltpu.VMEM((fold, slots), F32),
            pltpu.VMEM((virt_count, 2 * slots), BF16),
            pltpu.VMEM((virt_count, 2 * slots), BF16),
            pltpu.VMEM((virt_count, aux_width), F32),
            pltpu.SemaphoreType.DMA((bands,)),
        ],
        compiler_params=params,
    )(*evens, *odds, first, left, right, back, gap, x_high, x_low)
    return density.reshape(1, virt_count, aux_width)


def per_device(occupied_integrals, virtual_coefficients, *rest):
    blk_count = lax.axis_size("blk")
    slots, virt_count = virtual_coefficients.shape
    paired = blk_count % 2 == 0 and blk_count == occupied_integrals.shape[0]
    parts = lax.axis_size("aux")
    shared = parts > 1 and parts & (parts - 1) == 0 and slots % 128 == 0 and slots <= virt_count
    run = slots_first if paired and shared else transformed_first
    return run(occupied_integrals, virtual_coefficients, *rest)


def solution(mesh):
    in_specs = (P(None, "blk", "aux"), P(), P(), P(), P(), P(), P())
    out_specs = P("blk", None, "aux")
    return jax.shard_map(
        per_device, mesh=mesh, in_specs=in_specs, out_specs=out_specs, check_vma=False
    )
```

```python
import functools

import jax
import jax.numpy as jnp
from jax import lax
from jax.experimental import pallas as pl
from jax.experimental.pallas import tpu as pltpu
from jax.sharding import PartitionSpec as P

STOPS = 3
BF16 = jnp.bfloat16
F32 = jnp.float32


def shifted(value, axis, steps):
    count = lax.axis_size(axis)
    pairs = [(source, (source + steps) % count) for source in range(count)]
    return lax.ppermute(value, axis, pairs)


def swapped(value, axis, step):
    return lax.ppermute(value, axis, [(i, i ^ step) for i in range(lax.axis_size(axis))])


def live_slots(shell_size, shell_owner, blk_count, slot_cap):
    owner_hits = (shell_owner[:, None] == jnp.arange(blk_count, dtype=jnp.int32)[None, :]).astype(
        jnp.int32
    )
    slot_load = jnp.sum(shell_size[:, None] * owner_hits, axis=0)
    return (jnp.arange(slot_cap, dtype=jnp.int32)[None, :] < slot_load[:, None]).astype(F32)


def transformed_first(
    occupied_integrals, virtual_coefficients, shell_size, shell_owner, occ_owner, e_occ, e_virt
):
    blk_count = lax.axis_size("blk")
    occ_total = occupied_integrals.shape[0]
    slot_cap = occupied_integrals.shape[1]
    aux_width = occupied_integrals.shape[2]
    virt_count = virtual_coefficients.shape[1]
    occ_local = occ_total // blk_count
    pair_rows = occ_local * virt_count
    highest = lax.Precision.HIGHEST
    live_mask = live_slots(shell_size, shell_owner, blk_count, slot_cap)
    masked_coef = (
        virtual_coefficients.reshape(blk_count, slot_cap, virt_count) * live_mask[:, :, None]
    )
    grouped = jnp.take(occupied_integrals, occ_owner, axis=0).reshape(
        blk_count, occ_local, slot_cap, aux_width
    )
    owned = jnp.einsum(
        "dnkq,dkv->nvq",
        lax.all_to_all(grouped, "blk", split_axis=0, concat_axis=0, tiled=True),
        masked_coef,
        precision=highest,
    )
    own_block = owned.reshape(pair_rows, aux_width)
    my_index = lax.axis_index("blk")
    block_energy = jnp.take(e_occ, occ_owner).reshape(blk_count, occ_local)
    own_energy = lax.dynamic_index_in_dim(block_energy, my_index, 0, keepdims=False)
    partners = [own_block]
    partner_energies = [own_energy]
    passing = own_block
    for stop in range(1, STOPS):
        passing = shifted(passing, "blk", 1)
        partners.append(passing)
        partner_index = jnp.mod(my_index - stop, blk_count)
        partner_energies.append(
            lax.dynamic_index_in_dim(block_energy, partner_index, 0, keepdims=False)
        )
    density = jnp.zeros((pair_rows, aux_width), F32)
    for stop in range(STOPS):
        pair_ints = jnp.einsum("rq,cq->rc", own_block, partners[stop], precision=highest)
        pair_ints = pair_ints.reshape(occ_local, virt_count, occ_local, virt_count)
        summed = lax.psum(2.0 * pair_ints - pair_ints.transpose(0, 3, 2, 1), "aux")
        amplitudes = (
            summed
            / (
                own_energy[:, None, None, None]
                + partner_energies[stop][None, None, :, None]
                - e_virt[None, :, None, None]
                - e_virt[None, None, None, :]
            )
        ).reshape(pair_rows, pair_rows)
        density = density + jnp.dot(amplitudes, partners[stop], precision=highest)
    return density.reshape(occ_local, virt_count, aux_width)


def halves(value):
    high = value.astype(BF16)
    return high, (value - high.astype(F32)).astype(BF16)


def matmul(a, b):
    return jnp.dot(a, b, preferred_element_type=F32)


def matmul_nt(a, b):
    return lax.dot_general(a, b, (((1,), (1,)), ((), ())), preferred_element_type=F32)


def partner_chip(chip, step, chips):
    return chip ^ step if chips & (chips - 1) == 0 else lax.rem(chip + step, chips)


def source_chip(chip, step, chips):
    return chip ^ step if chips & (chips - 1) == 0 else lax.rem(chip + chips - step, chips)


def select_kernel(blk_count, owner_hbm, x_hbm, *refs):
    *outs, owner_ref, x_ref, owner_sem, x_sem = refs
    chips = blk_count // 2
    me = lax.axis_index("blk")
    my_chip, my_core = me >> 1, me & 1
    reads = [
        pltpu.make_async_copy(owner_hbm, owner_ref, owner_sem),
        pltpu.make_async_copy(x_hbm, x_ref, x_sem),
    ]
    for read in reads:
        read.start()
    for read in reads:
        read.wait()

    def rows(block):
        return x_ref[owner_ref[lax.rem(block + blk_count, blk_count)]]

    for step in range(chips):
        last = 2 * partner_chip(my_chip, step, chips)
        mine, theirs = last - 2 + 3 * my_core, last - 2 + 3 * (1 - my_core)
        whole = outs[2 * step]
        whole[0], whole[1] = rows(last), rows(last - 1)
        if step == chips - 1:
            whole[2], whole[3] = rows(last + 1), rows(last - 2)
            continue
        whole[2] = rows(mine)
        rest = outs[2 * step + 1]
        if step == 0:
            rest[0], rest[1] = whole[0], whole[1]
        rest[rest.shape[0] - 1] = rows(theirs)


def coefficient_kernel(
    blk_count,
    size_ref,
    shell_ref,
    owner_ref,
    energy_ref,
    coef_ref,
    virt_ref,
    left_ref,
    right_ref,
    back_ref,
    gap_ref,
    ordered,
):
    slots = coef_ref.shape[0]
    slot_cap = slots // blk_count
    me = lax.axis_index("blk")
    shells = [(size_ref[s], shell_ref[s]) for s in range(size_ref.shape[0])]
    count = lax.broadcasted_iota(jnp.int32, (slot_cap, coef_ref.shape[1]), 0)
    for index in range(blk_count):
        chip = source_chip(me >> 1, index // 2, blk_count // 2)
        blk = 2 * chip + ((me & 1) ^ (index % 2))
        load = jnp.int32(0)
        for size, shell in shells:
            load = load + jnp.where(shell == blk, size, 0)
        rows = coef_ref[pl.ds(pl.multiple_of(blk * slot_cap, slot_cap), slot_cap), :]
        ordered[pl.ds(index * slot_cap, slot_cap), :] = jnp.where(count < load, rows, 0.0)
    coef = ordered[...]
    high, low = halves(coef)
    right_ref[...] = jnp.concatenate([high, low, high], axis=0)
    turned = coef.T
    high, low = halves(turned)
    left_ref[...] = jnp.concatenate([high, high, low], axis=1)
    back_ref[...] = jnp.concatenate([high, low], axis=1)
    row = virt_ref[...]
    virt_count = row.shape[1]
    column = jnp.broadcast_to(row, (8, virt_count)).T[:, :1]
    own = energy_ref[owner_ref[me]]
    for stop in range(STOPS):
        both = own + energy_ref[owner_ref[lax.rem(me + blk_count - stop, blk_count)]]
        gap_ref[pl.ds(stop * virt_count, virt_count), :] = 1.0 / ((both - column) - row)


def join_kernel(*refs):
    *pieces, out = refs
    for index, piece in enumerate(pieces):
        out[index] = piece[0]


def overlap_kernel(slot_cap, layout, *refs):
    *operands, keep, give, x_high, x_low, total, folded = refs
    count = 1 + max(place for entries in layout for _, _, place in entries)
    my_core = lax.axis_index("blk") & 1
    here = lax.axis_index("aux")
    for entries, operand in zip(layout, operands):
        for row, offset, place in entries:
            stop = lax.rem(offset + my_core, STOPS)
            high, low = halves(operand[3 - my_core if row == 3 else row])
            target = pl.ds(pl.multiple_of((stop * count + place) * slot_cap, slot_cap), slot_cap)
            x_high[target, :] = high
            x_low[target, :] = low
    slots = slot_cap * count
    own = jnp.concatenate([x_high[:slots, :], x_low[:slots, :]], axis=0)
    both = matmul_nt(own, x_high[...])
    gram = both[:slots] + both[slots:] + matmul_nt(x_high[:slots, :], x_low[...])
    half, band, thin = slots // 2, slots // 4, slots // 8
    for stop in range(1, STOPS):
        square = gram[:, stop * slots : (stop + 1) * slots]
        total[stop - 1] = 2.0 * square - square.T
    square = gram[:, :slots]
    lanes = lax.broadcasted_iota(jnp.int32, (band, slots), 1)
    folded[:band, :] = square[:band]
    folded[band:half, :] = jnp.where(
        lanes < band, pltpu.roll(square[half + band :], band, 1), square[band:half]
    )
    folded[half:, :] = jnp.where(
        lanes[:thin] < half,
        pltpu.roll(square[half + thin : half + band], half, 1),
        square[half : half + thin],
    )
    rest = folded.shape[0] // 2
    for out, part in ((keep, here & 1), (give, 1 - (here & 1))):
        packed = folded[pl.ds(pl.multiple_of(part * rest, 8), rest), :]
        out[...] = jnp.concatenate([total[part], packed], axis=0)


def weigh(total, left, right, back, gap, w_high, w_low):
    slots = total.shape[0]
    virt_count = w_high.shape[0]
    stops = total.shape[1] // slots
    high, low = halves(total)
    half_done = matmul(left[...], jnp.concatenate([high, low, high], axis=0))
    half_done = jnp.concatenate(
        [half_done[:, stop * slots : (stop + 1) * slots] for stop in range(stops)], axis=0
    )
    high, low = halves(half_done)
    summed = matmul(jnp.concatenate([high, high, low], axis=1), right[...])
    high, low = halves(summed * gap)
    both = matmul(high, back[...])
    weight = both[:, :slots] + both[:, slots:] + matmul(low, back[:, :slots])
    for stop in range(stops):
        cols = slice(stop * slots, (stop + 1) * slots)
        w_high[:, cols], w_low[:, cols] = halves(
            weight[stop * virt_count : (stop + 1) * virt_count]
        )


def rows_of(ref, stop, count):
    return ref[pl.ds(pl.multiple_of(stop * count, count), count), :]


def first_density_kernel(*refs):
    *shares, left, right, back, gap, x_high, x_low, out, w_high, w_low = refs
    slots = left.shape[1] // 3
    stop = 1 + (lax.axis_index("aux") & 1)
    square = sum(piece[:slots, :] for piece in shares)
    weigh(square, left, right, back, rows_of(gap, stop, out.shape[0]), w_high, w_low)
    high, low = rows_of(x_high, stop, slots), rows_of(x_low, stop, slots)
    x_all = jnp.concatenate([high, high, low], axis=0)
    out[...] = matmul(jnp.concatenate([w_high[...], w_low[...], w_high[...]], axis=1), x_all)


def last_density_kernel(count, *refs):
    first, second = refs[:count], refs[count : 2 * count]
    before, left, right, back, gap, x_high, x_low, out, *scratch = refs[2 * count :]
    total, folded, w_high, w_low, density, sems = scratch
    mine = lax.axis_index("aux") & 1
    stop = 2 - mine
    slots = total.shape[0]
    half = slots // 2
    band, rest = slots // 4, folded.shape[0] // 2
    virt_count = out.shape[0]
    for part, pieces in ((mine, first), (1 - mine, second)):
        folded[pl.ds(pl.multiple_of(part * rest, 8), rest), :] = sum(
            piece[slots:, :] for piece in pieces
        )
    total[:, slots:] = sum(piece[:slots, :] for piece in second)
    last = folded[half:, :]
    upper = jnp.concatenate(
        [
            folded[:half, :],
            last,
            pltpu.roll(last, half, 1),
            pltpu.roll(folded[band:half, :], slots - band, 1),
        ],
        axis=0,
    )
    row_band = lax.broadcasted_iota(jnp.int32, (slots, slots), 0) // band
    lane_band = lax.broadcasted_iota(jnp.int32, (slots, slots), 1) // band
    total[:, :slots] = jnp.where(lane_band >= row_band, upper, upper.T)
    gaps = jnp.concatenate([gap[:virt_count, :], rows_of(gap, stop, virt_count)], axis=0)
    weigh(total[...], left, right, back, gaps, w_high, w_low)
    x_high = jnp.concatenate([x_high[:slots, :], rows_of(x_high, stop, slots)], axis=0)
    x_low = jnp.concatenate([x_low[:slots, :], rows_of(x_low, stop, slots)], axis=0)
    copies = []
    for index in range(sems.shape[0]):
        band = virt_count // sems.shape[0]
        rows = pl.ds(index * band, band)
        high, low = w_high[rows, :], w_low[rows, :]
        both = matmul(jnp.concatenate([high, low], axis=0), x_high)
        density[rows, :] = before[rows, :] + both[:band] + both[band:] + matmul(high, x_low)
        copies.append(pltpu.make_async_copy(density.at[rows], out.at[rows], sems.at[index]))
        copies[-1].start()
    for copy in copies:
        copy.wait()


def slots_first(
    occupied_integrals, virtual_coefficients, shell_size, shell_owner, occ_owner, e_occ, e_virt
):
    blk_count = lax.axis_size("blk")
    parts = lax.axis_size("aux")
    _, slot_cap, aux_width = occupied_integrals.shape
    slots, virt_count = virtual_coefficients.shape
    chips = blk_count // 2
    vmem = pl.BlockSpec(memory_space=pltpu.VMEM)
    smem = pl.BlockSpec(memory_space=pltpu.SMEM)
    params = pltpu.CompilerParams(vmem_limit_bytes=24 * 1024 * 1024)

    def block(count):
        return jax.ShapeDtypeStruct((count, slot_cap, aux_width), F32)

    sent = pl.pallas_call(
        functools.partial(select_kernel, blk_count),
        out_shape=[block(STOPS)] * 2 + [block(STOPS), block(1)] * (chips - 2) + [block(4)],
        in_specs=[pl.BlockSpec(memory_space=pltpu.HBM)] * 2,
        out_specs=[vmem] * (2 * chips - 1),
        scratch_shapes=[
            pltpu.SMEM(occ_owner.shape, jnp.int32),
            pltpu.VMEM(occupied_integrals.shape, F32),
            pltpu.SemaphoreType.DMA,
            pltpu.SemaphoreType.DMA,
        ],
        compiler_params=params,
    )(*[pltpu.with_memory_space_constraint(a, pltpu.HBM) for a in (occ_owner, occupied_integrals)])

    def entries(place, rows=STOPS):
        return [(row, row, place) for row in range(rows)]

    own = [(sent[0], entries(0)), (swapped(sent[1], "blk", 1), entries(1))]
    whole, rest = [], []
    for step in range(1, chips):
        ways = [
            [
                (2 * chip + core, 2 * int(partner_chip(chip, step, chips)) + (core ^ cross))
                for chip in range(chips)
                for core in range(2)
            ]
            for cross in range(2)
        ]
        piece = lax.ppermute(sent[2 * step], "blk", ways[0])
        if step == chips - 1:
            both = [[*entries(place, 2), (3, 2, place)] for place in (2 * step, 2 * step + 1)]
            held, sibling = lax.optimization_barrier((piece, own[1][0]))
            own[1] = (sibling, own[1][1])
            whole += [(piece, both[0]), (swapped(held, "blk", 1), both[1])]
            continue
        other = lax.ppermute(sent[2 * step + 1], "blk", ways[1])
        whole.append((piece, entries(2 * step)))
        whole.append((swapped(piece, "blk", 1), entries(2 * step + 1, 2)))
        rest.append(other)
    joined = pl.pallas_call(
        join_kernel,
        out_shape=block(chips - 2),
        in_specs=[vmem] * (chips - 2),
        out_specs=vmem,
        compiler_params=params,
        cost_estimate=pl.CostEstimate(flops=2 * 10**9, bytes_accessed=0, transcendentals=0),
    )(*rest)
    last = [(joined, [(row, 2, 2 * step + 1) for row, step in enumerate(range(1, chips - 1))])]
    farthest_first = [whole[2 * step - 2 + one] for step in range(chips - 1, 0, -1) for one in (0, 1)]
    pieces = farthest_first + own + last
    operands, layout = zip(*pieces)

    left, right, back, gap = pl.pallas_call(
        functools.partial(coefficient_kernel, blk_count),
        out_shape=[
            jax.ShapeDtypeStruct((virt_count, 3 * slots), BF16),
            jax.ShapeDtypeStruct((3 * slots, virt_count), BF16),
            jax.ShapeDtypeStruct((virt_count, 2 * slots), BF16),
            jax.ShapeDtypeStruct((STOPS * virt_count, virt_count), F32),
        ],
        in_specs=[smem] * 4 + [vmem] * 2,
        out_specs=[vmem] * 4,
        scratch_shapes=[pltpu.VMEM((slots, virt_count), F32)],
        compiler_params=params,
    )(
        shell_size,
        shell_owner,
        occ_owner,
        e_occ,
        virtual_coefficients,
        e_virt.reshape(1, virt_count),
    )

    fold = 5 * slots // 8
    keep, give, x_high, x_low = pl.pallas_call(
        functools.partial(overlap_kernel, slot_cap, layout),
        out_shape=[jax.ShapeDtypeStruct((slots + fold // 2, slots), F32)] * 2
        + [jax.ShapeDtypeStruct((STOPS * slots, aux_width), BF16)] * 2,
        in_specs=[vmem] * len(operands),
        out_specs=[vmem] * 4,
        scratch_shapes=[
            pltpu.VMEM((STOPS - 1, slots, slots), F32),
            pltpu.VMEM((fold, slots), F32),
        ],
        compiler_params=params,
    )(*operands)

    taken = swapped(give, "aux", 1)
    mine = keep + taken
    mine, left = lax.optimization_barrier((mine, left))
    evens = [mine] + [swapped(mine, "aux", step) for step in range(2, parts, 2)]
    held = mine
    odds = [swapped(held, "aux", step) for step in range(1, parts, 2)]
    bands = 3 if virt_count % 48 == 0 else 1
    flops = 18 * virt_count * slots * (slots + 2 * virt_count + aux_width)

    first = pl.pallas_call(
        first_density_kernel,
        out_shape=jax.ShapeDtypeStruct((virt_count, aux_width), F32),
        in_specs=[vmem] * (len(evens) + 6),
        out_specs=vmem,
        scratch_shapes=[pltpu.VMEM((virt_count, slots), BF16)] * 2,
        compiler_params=params,
        cost_estimate=pl.CostEstimate(flops=flops, bytes_accessed=0, transcendentals=0),
    )(*evens, left, right, back, gap, x_high, x_low)
    density = pl.pallas_call(
        functools.partial(last_density_kernel, len(evens)),
        out_shape=jax.ShapeDtypeStruct((virt_count, aux_width), F32),
        in_specs=[vmem] * (len(evens) + len(odds) + 7),
        out_specs=pl.BlockSpec(memory_space=pl.ANY),
        scratch_shapes=[
            pltpu.VMEM((slots, 2 * slots), F32),
            pltpu.VMEM((fold, slots), F32),
            pltpu.VMEM((virt_count, 2 * slots), BF16),
            pltpu.VMEM((virt_count, 2 * slots), BF16),
            pltpu.VMEM((virt_count, aux_width), F32),
            pltpu.SemaphoreType.DMA((bands,)),
        ],
        compiler_params=params,
    )(*evens, *odds, first, left, right, back, gap, x_high, x_low)
    return density.reshape(1, virt_count, aux_width)


def per_device(occupied_integrals, virtual_coefficients, *rest):
    blk_count = lax.axis_size("blk")
    slots, virt_count = virtual_coefficients.shape
    paired = blk_count % 2 == 0 and blk_count > 4 and blk_count == occupied_integrals.shape[0]
    parts = lax.axis_size("aux")
    shared = parts > 1 and parts & (parts - 1) == 0 and slots % 128 == 0 and slots <= virt_count
    run = slots_first if paired and shared else transformed_first
    return run(occupied_integrals, virtual_coefficients, *rest)


def solution(mesh):
    in_specs = (P(None, "blk", "aux"), P(), P(), P(), P(), P(), P())
    out_specs = P("blk", None, "aux")
    return jax.shard_map(
        per_device, mesh=mesh, in_specs=in_specs, out_specs=out_specs, check_vma=False
    )
```
